32 devices in a mesh: wide: 16 (over z, y, core), narrow: 2 (over x).
Axes of the slice: x: 2, y: 2, z: 4, core: 2. Of those that a mesh axis runs over, the one named last changes fastest.
Arguments:
- hidden_in: bfloat16 [4096, 2048], P('wide', 'narrow'), may hold values from -64 to 64
- cache_lengths: int32 [32], P('wide'), may hold values from 1 to 1023, as said below
- cache_offsets: int32 [32], P('wide'), may hold values from 0 to 16383, as said below
- cache_kv: bfloat16 [2, 2, 16384, 2048], P(None, None, 'wide', 'narrow'), may hold values from -16 to 16
- w_qkv: bfloat16 [2048, 3, 2048], P('wide', None, 'narrow'), may hold values from -0.125 to 0.125
- qkv_bias: bfloat16 [3, 2048], P(None, 'narrow'), may hold values from -40 to 40
- w_out: bfloat16 [2048, 2048], P('wide', 'narrow'), may hold values from -0.125 to 0.125
- out_bias: bfloat16 [2048], P('narrow'), may hold values from -3 to 3
- norm_gain: bfloat16 [2048], P('narrow'), may hold values from 0.2 to 5
- norm_shift: bfloat16 [2048], P('narrow'), may hold values from -3 to 3
Outputs:
- hidden_out: bfloat16 [4096, 2048], P('wide', 'narrow')
- new_cache: bfloat16 [2, 2, 4096, 2048], P(None, None, 'wide', 'narrow')
The draws below stay inside these ranges and needn't reach their ends.
Inputs may be any that keep to these rules, and one draw needn't show every extreme that they name: `cache_lengths`: the cached lengths of the 2 requests r with the same r // 2 sum to at most 1024; for some such group exactly 1024, and in it one request has 1023 rows. Request r's cache is rows cache_offsets[r] to cache_offsets[r] + cache_lengths[r] - 1 of the packed cache, all within rows (r // 2) * 1024 to (r // 2 + 1) * 1024 - 1; the row ranges of different requests are disjoint.
All inputs are finite; a program needn't handle non-finite values.
Results may differ from the reference program's by a relative error of at most 0.02.
Values may be sent and summed in bfloat16 or wider, within the bound.
A program may use at most 128 MiB of HBM per device.

```python
import math
import jax
import jax.numpy as jnp
from jax import lax

HEADS = 16
HEAD = 128
D = 2048
SPAN = 128
REQ_DEV = 2
CACHE_DEV = 1024
LAYERS = 2
REQUESTS = 32
TOKENS = 4096
CACHE_ROWS = 16384


def layout_helper(key):
    base = jax.random.fold_in(key, 4242)
    keys = jax.random.split(base, 6)
    groups = REQUESTS // REQ_DEV
    shifts = jax.random.randint(keys[0], (groups,), 0, 4)
    capacity = jnp.right_shift(jnp.full((groups,), CACHE_DEV, jnp.int32), shifts)
    reduction = jax.random.randint(keys[1], (groups,), 0, 1 << 20) % (capacity // 4 + 1)
    totals = jnp.maximum(capacity - reduction, REQ_DEV)
    chosen = jax.random.randint(keys[2], (), 0, groups)
    is_chosen = jnp.arange(groups) == chosen
    totals = jnp.where(is_chosen, CACHE_DEV, totals).astype(jnp.int32)
    shares = jax.random.randint(keys[3], (groups, REQ_DEV), 1, 65536)
    lengths = 1 + (totals - REQ_DEV)[:, None] * shares // jnp.sum(shares, axis=1, keepdims=True)
    lengths = lengths.at[:, -1].set(totals - jnp.sum(lengths[:, :-1], axis=1))
    heavy = jnp.where(jnp.arange(REQ_DEV) == REQ_DEV - 1, CACHE_DEV - REQ_DEV + 1, 1).astype(lengths.dtype)
    lengths = jnp.where(is_chosen[:, None], heavy[None, :], lengths)
    ranking = jax.random.randint(keys[4], (groups, REQ_DEV), 0, 1 << 20) * REQ_DEV + jnp.arange(REQ_DEV)[None, :]
    order = jnp.argsort(ranking, axis=1)
    stored_lengths = jnp.take_along_axis(lengths, order, axis=1)
    leading_gap = jax.random.randint(keys[5], (groups,), 0, 1 << 20) % (CACHE_DEV - totals + 1)
    stored_starts = leading_gap[:, None] + jnp.cumsum(stored_lengths, axis=1) - stored_lengths
    inverse = jnp.argsort(order, axis=1)
    starts = jnp.take_along_axis(stored_starts, inverse, axis=1) + (jnp.arange(groups) * CACHE_DEV)[:, None]
    return (lengths.reshape(-1).astype(jnp.int32), starts.reshape(-1).astype(jnp.int32))


def draw_cache_lengths(key, part):
    lengths, starts = layout_helper(key)
    return lengths


def draw_cache_offsets(key, part):
    lengths, starts = layout_helper(key)
    return starts


def draw_hidden_in(key, part):
    keys = jax.random.split(jax.random.fold_in(key, 3), 3)
    position = jnp.arange(D, dtype=jnp.float32) / (D - 1)
    column_scale = jnp.exp(math.log(0.3) + math.log(10.0) * position) * jax.random.uniform(keys[0], (D,), jnp.float32, 0.7, 1.4)
    row_scale = jnp.exp(jax.random.uniform(keys[1], (TOKENS, 1), jnp.float32, math.log(0.3), math.log(3.0)))
    noise = jnp.clip(jax.random.normal(keys[2], (TOKENS, D), jnp.float32), -4.0, 4.0)
    return (noise * column_scale[None, :] * row_scale).astype(jnp.bfloat16)


def draw_cache_kv(key, part):
    shape = (LAYERS, 2, CACHE_ROWS, D)
    noise_key = jax.random.fold_in(key, 5)
    values = jnp.clip(jax.random.normal(noise_key, shape, jnp.float32), -6.0, 6.0)
    return values.astype(jnp.bfloat16)


def draw_qkv_bias(key, part):
    values = 0.5 * jnp.clip(jax.random.normal(jax.random.fold_in(key, 1), (3, D), jnp.float32), -6.0, 6.0)
    return values.astype(jnp.bfloat16)


def draw_norm_gain(key, part):
    position = jnp.arange(D, dtype=jnp.float32) / (D - 1)
    rising = jnp.exp(math.log(0.5) + math.log(6.0) * position)
    jitter = jax.random.uniform(jax.random.fold_in(key, 2), (D,), jnp.float32, 0.75, 1.33)
    return (rising * jitter).astype(jnp.bfloat16)


def block_levels(stream_key, dims, pieces, smallest, largest):
    factor_of = 1.0
    for dim, parts in pieces:
        steps = jax.random.uniform(jax.random.fold_in(jax.random.fold_in(stream_key, 6), dim), (parts,), jnp.float32, smallest / len(pieces), largest / len(pieces))
        factor_of = factor_of * jnp.repeat(jnp.exp(steps), dims[dim] // parts).reshape((-1,) + (1,) * (len(dims) - 1 - dim))
    return factor_of


def bell_draw(own_key, shape, deviation, reach, cuts=(), held_as=jnp.bfloat16):
    values = deviation * jax.random.normal(own_key, shape, jnp.float32)
    if cuts:
        values = values * block_levels(own_key, shape, cuts, -0.22, 0.18)
    return jnp.clip(values, -reach, reach).astype(held_as)


def setup_inputs(seed: int = 0) -> dict:
    key_of = jax.random.split(jax.random.key(seed), 11)
    return {
        "hidden_in": draw_hidden_in(jax.random.fold_in(key_of[10], 71), 0),
        "cache_lengths": draw_cache_lengths(jax.random.fold_in(key_of[10], 71), 0),
        "cache_offsets": draw_cache_offsets(jax.random.fold_in(key_of[10], 71), 0),
        "cache_kv": draw_cache_kv(jax.random.fold_in(key_of[10], 71), 0),
        "w_qkv": bell_draw(key_of[4], (D, 3, D), D ** -0.5, 0.125, ((0, 16), (2, 2))),
        "qkv_bias": draw_qkv_bias(jax.random.fold_in(key_of[10], 71), 0),
        "w_out": bell_draw(key_of[6], (D, D), D ** -0.5, 0.125, ((0, 16), (1, 2))),
        "out_bias": bell_draw(key_of[7], (D,), 0.5, 3.0, ((0, 2),)),
        "norm_gain": draw_norm_gain(jax.random.fold_in(key_of[10], 71), 0),
        "norm_shift": bell_draw(key_of[9], (D,), 0.5, 3.0, ((0, 2),)),
    }


EPSILON = 1e-05
NEGATIVE = -1e+30

def normalize(summed, norm_gain, norm_shift):
    values = summed.astype(jnp.float32)
    row_means = lax.optimization_barrier(jnp.mean(values, axis=1, keepdims=True))
    centered = values - row_means
    row_spread = lax.optimization_barrier(jnp.mean(centered * centered, axis=1, keepdims=True))
    scaled = centered * lax.rsqrt(row_spread + EPSILON)
    return (scaled * norm_gain.astype(jnp.float32) + norm_shift.astype(jnp.float32)).astype(jnp.bfloat16)

def reference(hidden_in, cache_lengths, cache_offsets, cache_kv, w_qkv, qkv_bias, w_out, out_bias, norm_gain, norm_shift):
    scale_factor = 1.0 / HEAD ** 0.5
    qkv_flat = w_qkv.reshape(D, 3 * D)
    bias_flat = qkv_bias.astype(jnp.float32).reshape(3 * D)
    causal = jnp.arange(SPAN)[:, None] >= jnp.arange(SPAN)[None, :]
    layer_input = hidden_in
    appended = []
    for layer_index in range(LAYERS):
        projections = jnp.dot(layer_input, qkv_flat, preferred_element_type=jnp.float32) + bias_flat
        queries = projections[:, :D].astype(jnp.bfloat16)
        keys_new = projections[:, D:2 * D].astype(jnp.bfloat16)
        values_new = projections[:, 2 * D:].astype(jnp.bfloat16)
        appended.append(jnp.stack([keys_new, values_new]))
        cache_keys = cache_kv[layer_index, 0]
        cache_values = cache_kv[layer_index, 1]

        def attend_one(request):
            block_start = (request // REQ_DEV * CACHE_DEV).astype(jnp.int32)
            token_start = (request * SPAN).astype(jnp.int32)
            keys_block = lax.dynamic_slice_in_dim(cache_keys, block_start, CACHE_DEV, 0).reshape(CACHE_DEV, HEADS, HEAD)
            values_block = lax.dynamic_slice_in_dim(cache_values, block_start, CACHE_DEV, 0).reshape(CACHE_DEV, HEADS, HEAD)
            query_rows = lax.dynamic_slice_in_dim(queries, token_start, SPAN, 0).reshape(SPAN, HEADS, HEAD)
            keys_fresh = lax.dynamic_slice_in_dim(keys_new, token_start, SPAN, 0).reshape(SPAN, HEADS, HEAD)
            values_fresh = lax.dynamic_slice_in_dim(values_new, token_start, SPAN, 0).reshape(SPAN, HEADS, HEAD)
            rows_global = block_start + jnp.arange(CACHE_DEV, dtype=jnp.int32)
            row_start = cache_offsets[request]
            row_stop = row_start + cache_lengths[request]
            live_rows = (rows_global >= row_start) & (rows_global < row_stop)
            mask_all = jnp.concatenate([jnp.broadcast_to(live_rows[None, :], (SPAN, CACHE_DEV)), causal], axis=1)
            keys_all = jnp.concatenate([keys_block, keys_fresh], axis=0).astype(jnp.float32)
            values_all = jnp.concatenate([values_block, values_fresh], axis=0).astype(jnp.float32)
            scores = jnp.einsum('qhd,khd->hqk', query_rows.astype(jnp.float32), keys_all) * scale_factor
            masked = jnp.where(mask_all[None], scores, NEGATIVE)
            top_score = lax.optimization_barrier(jnp.max(masked, axis=2, keepdims=True))
            weights = jnp.where(mask_all[None], jnp.exp(masked - top_score), 0.0)
            probabilities = (weights / lax.optimization_barrier(jnp.sum(weights, axis=2, keepdims=True))).astype(jnp.bfloat16)
            combined = jnp.einsum('hqk,khd->qhd', probabilities.astype(jnp.float32), values_all)
            return combined.astype(jnp.bfloat16).reshape(SPAN, D)
        attended = lax.map(attend_one, jnp.arange(REQUESTS, dtype=jnp.int32)).reshape(TOKENS, D)
        projected = jnp.dot(attended, w_out, preferred_element_type=jnp.float32) + out_bias.astype(jnp.float32)
        summed = (projected + layer_input.astype(jnp.float32)).astype(jnp.bfloat16)
        layer_input = normalize(summed, norm_gain, norm_shift)
    return (layer_input, jnp.stack(appended))
```

```python
import functools
import math

import jax
import jax.numpy as jnp
from jax import lax
from jax.experimental import pallas as pl
from jax.experimental.pallas import tpu as pltpu
from jax.sharding import PartitionSpec as P

HEAD = 128
SPAN = 128
LAYERS = 2


EPSILON = 1e-05
NEGATIVE = -1e30


def add_rows(shard_piece, operand):
    piece_rows = shard_piece.shape[0]
    return jnp.dot(operand, shard_piece.reshape(piece_rows, -1), preferred_element_type=jnp.float32)


def norm_slice(summed, norm_gain, norm_shift, full_width):
    values = summed.astype(jnp.float32)
    row_means = lax.psum(jnp.sum(values, axis=1), "narrow") / full_width
    centered = values - row_means[:, None]
    row_spread = lax.psum(jnp.sum(centered * centered, axis=1), "narrow") / full_width
    scaled = centered * lax.rsqrt(row_spread[:, None] + EPSILON)
    return (scaled * norm_gain.astype(jnp.float32) + norm_shift.astype(jnp.float32)).astype(
        jnp.bfloat16
    )


def attend(queries, keys_new, values_new, keys_cache, values_cache, live_cache, live_new):
    scale_factor = 1.0 / math.sqrt(queries.shape[2])
    scores_cache = (
        jnp.einsum("qhd,khd->hqk", queries, keys_cache, preferred_element_type=jnp.float32)
        * scale_factor
    )
    scores_new = (
        jnp.einsum("qhd,khd->hqk", queries, keys_new, preferred_element_type=jnp.float32)
        * scale_factor
    )
    masked_cache = jnp.where(live_cache[None], scores_cache, NEGATIVE)
    masked_new = jnp.where(live_new[None], scores_new, NEGATIVE)
    top_score = jnp.maximum(jnp.max(masked_cache, axis=2), jnp.max(masked_new, axis=2))[:, :, None]
    weights_cache = jnp.where(live_cache[None], jnp.exp(masked_cache - top_score), 0.0)
    weights_new = jnp.where(live_new[None], jnp.exp(masked_new - top_score), 0.0)
    totals = jnp.sum(weights_cache, axis=2, keepdims=True) + jnp.sum(
        weights_new, axis=2, keepdims=True
    )
    probs_cache = (weights_cache / totals).astype(jnp.bfloat16)
    probs_new = (weights_new / totals).astype(jnp.bfloat16)
    combined = jnp.einsum(
        "hqk,khd->qhd", probs_cache, values_cache, preferred_element_type=jnp.float32
    )
    combined = combined + jnp.einsum(
        "hqk,khd->qhd", probs_new, values_new, preferred_element_type=jnp.float32
    )
    return combined.astype(jnp.bfloat16).reshape(queries.shape[0], -1)


def shards(
    hidden_in,
    cache_lengths,
    cache_offsets,
    cache_kv,
    w_qkv,
    qkv_bias,
    w_out,
    out_bias,
    norm_gain,
    norm_shift,
):
    row_count, local_width = hidden_in.shape
    full_width = local_width * lax.axis_size("narrow")
    local_heads = local_width // HEAD
    cache_count = cache_kv.shape[2]
    requests_here = cache_lengths.shape[0]
    block_start = lax.axis_index("wide") * cache_count
    rows_global = block_start + jnp.arange(cache_count, dtype=jnp.int32)
    row_start = jnp.broadcast_to(cache_offsets[:, None], (requests_here, SPAN)).reshape(-1)
    row_stop = row_start + jnp.broadcast_to(cache_lengths[:, None], (requests_here, SPAN)).reshape(
        -1
    )
    live_cache = (rows_global[None, :] >= row_start[:, None]) & (
        rows_global[None, :] < row_stop[:, None]
    )
    owner_index = jnp.arange(row_count, dtype=jnp.int32) // SPAN
    position = jnp.arange(row_count, dtype=jnp.int32) % SPAN
    live_new = (owner_index[:, None] == owner_index[None, :]) & (
        position[:, None] >= position[None, :]
    )
    bias_flat = qkv_bias.astype(jnp.float32).reshape(-1)
    gathered = lax.all_gather(hidden_in, "narrow", axis=1, tiled=True)
    carried = hidden_in
    appended = []
    for layer_index in range(LAYERS):
        projections = add_rows(lax.all_gather(w_qkv, "wide", axis=0, tiled=True), operand=gathered)
        projections = projections + bias_flat
        queries = projections[:, :local_width].astype(jnp.bfloat16)
        keys_new = projections[:, local_width : 2 * local_width].astype(jnp.bfloat16)
        values_new = projections[:, 2 * local_width :].astype(jnp.bfloat16)
        appended.append(jnp.stack([keys_new, values_new]))
        keys_cache = cache_kv[layer_index, 0].reshape(cache_count, local_heads, HEAD)
        values_cache = cache_kv[layer_index, 1].reshape(cache_count, local_heads, HEAD)
        attended = attend(
            queries.reshape(row_count, local_heads, HEAD),
            keys_new.reshape(row_count, local_heads, HEAD),
            values_new.reshape(row_count, local_heads, HEAD),
            keys_cache,
            values_cache,
            live_cache,
            live_new,
        )
        heads_all = lax.all_gather(attended, "narrow", axis=1, tiled=True)
        projected = add_rows(lax.all_gather(w_out, "wide", axis=0, tiled=True), operand=heads_all)
        summed = (projected + out_bias.astype(jnp.float32) + carried.astype(jnp.float32)).astype(
            jnp.bfloat16
        )
        if layer_index + 1 < LAYERS:
            carried = norm_slice(summed, norm_gain, norm_shift, full_width)
            gathered = lax.all_gather(carried, "narrow", axis=1, tiled=True)
        else:
            carried = norm_slice(summed, norm_gain, norm_shift, full_width)
    return (carried, jnp.stack(appended))


MESH = pl.DeviceIdType.MESH
CHIPS_Y = 2
CHIPS_Z = 4
CORES = 2
UP, DOWN, ACROSS, SIBLING = range(4)
QKV, OUT = range(2)
FIRST, SECOND = range(2)
VMEM_BYTES = 58 * 1024 * 1024


def fits_fused(mesh):
    return mesh.shape["wide"] == CHIPS_Z * CHIPS_Y * CORES and mesh.shape["narrow"] == 2


class Gather:
    def __init__(self, buffers, shard_rows, cuts, send_sem, recv_sem):
        self.buffers, self.shard_rows, self.cuts = buffers, shard_rows, cuts
        self.send_sem, self.recv_sem = send_sem, recv_sem
        me = lax.axis_index("wide")
        self.core = lax.rem(me, CORES)
        self.y = lax.rem(me // CORES, CHIPS_Y)
        self.z = me // (CORES * CHIPS_Y)
        self.me = me
        self.targets = {
            UP: (self.z + 1 < CHIPS_Z, me + CORES * CHIPS_Y),
            DOWN: (self.z > 0, me - CORES * CHIPS_Y),
            ACROSS: (True, self.index(self.z, 1 - self.y, self.core)),
            SIBLING: (True, self.index(self.z, self.y, 1 - self.core)),
        }
        self.pending = []

    def index(self, z, y, core):
        return (z * CHIPS_Y + y) * CORES + core

    def slot(self, which, part, source):
        cut = self.cuts[which]
        start = source * self.shard_rows + (0 if part == FIRST else cut)
        size = cut if part == FIRST else self.shard_rows - cut
        return self.buffers[which].at[pl.ds(pl.multiple_of(start, 16), size), :]

    def copy(self, which, part, z, y, core, kind):
        source = self.index(z, y, core)
        block = self.slot(which, part, source)
        return pltpu.make_async_remote_copy(
            src_ref=block,
            dst_ref=block,
            send_sem=self.send_sem.at[which, part, z * CHIPS_Y + y, kind],
            recv_sem=self.recv_sem.at[which, part, source],
            device_id={"wide": self.targets[kind][1]},
            device_id_type=MESH,
        )

    def send(self, which, part, z, y, kinds, valid=True):
        for kind in kinds:
            condition = self.targets[kind][0]
            if condition is True:
                condition = valid
            elif valid is not True:
                condition = jnp.logical_and(condition, valid)
            make = functools.partial(self.copy, which, part, z, y, self.core, kind)
            self.when(condition, lambda make=make: make().start())
            self.pending.append((condition, make))

    def when(self, condition, action):
        if condition is True:
            action()
        else:
            pl.when(condition)(action)

    def arrive(self, which, part, z, y, core, valid=True):
        make = functools.partial(self.copy, which, part, z, y, core, SIBLING)
        self.when(valid, lambda: make().wait_recv())

    def begin(self, which):
        z, y = self.z, self.y
        self.send(which, SECOND, z, y, (ACROSS,))
        self.send(which, FIRST, z, y, (UP, DOWN, ACROSS))
        self.send(which, SECOND, z, y, (UP, DOWN))
        self.send(which, FIRST, z, y, (SIBLING,))
        self.send(which, SECOND, z, y, (SIBLING,))

    def around(self, distance):
        low, high = self.z - distance, self.z + distance
        return ((low, low >= 0, UP), (high, high < CHIPS_Z, DOWN))

    def take_across(self, which, distance):
        y = 1 - self.y
        places = ((self.z, True, None),) if distance == 0 else self.around(distance)
        for z, valid, _ in places:
            self.arrive(which, FIRST, z, y, self.core, valid)
            self.send(which, FIRST, z, y, (SIBLING,), valid)

    def step(self, which, distance):
        if distance == 0:
            y = 1 - self.y
            self.arrive(which, SECOND, self.z, y, self.core)
            self.send(which, SECOND, self.z, y, (UP, DOWN, SIBLING))
            return
        if distance < CHIPS_Z:
            for z, valid, onward in self.around(distance):
                self.arrive(which, FIRST, z, self.y, self.core, valid)
                self.send(which, FIRST, z, self.y, (onward, ACROSS, SIBLING), valid)
            for z, valid, onward in self.around(distance):
                for y in (self.y, 1 - self.y):
                    self.arrive(which, SECOND, z, y, self.core, valid)
                    self.send(which, SECOND, z, y, (onward, SIBLING), valid)
        self.take_across(which, distance - 1)

    def finish(self, which):
        for part in (FIRST, SECOND):
            for z in range(CHIPS_Z):
                for y in range(CHIPS_Y):
                    self.arrive(which, part, z, y, 1 - self.core)

    def drain(self):
        for condition, make in self.pending:
            self.when(condition, lambda make=make: make().wait_send())


def fused_kernel(
    lengths,
    offsets,
    hidden,
    cache,
    w_qkv,
    w_out,
    qkv_bias,
    out_bias,
    scales,
    hidden_out,
    new_cache,
    qkv_rows,
    out_rows,
    cache_here,
    inputs,
    projected,
    attended,
    summed,
    normed,
    scales_all,
    stats,
    live,
    send_sem,
    recv_sem,
    local_sem,
    side_send,
    side_recv,
):
    tokens, width = hidden.shape
    cache_count = cache.shape[2]
    requests = lengths.shape[0]
    shard_rows = w_qkv.shape[0]
    heads = width // HEAD
    full_width = 2 * width
    column = lax.axis_index("narrow")
    other = 1 - column
    gather = Gather((qkv_rows, out_rows), shard_rows, (112, 96), send_sem, recv_sem)

    barrier = pltpu.get_barrier_semaphore()
    for condition, target in gather.targets.values():

        def greet(target=target):
            pl.semaphore_signal(
                barrier, inc=1, device_id={"wide": target}, device_id_type=MESH
            )

        gather.when(condition, greet)
    pl.semaphore_signal(barrier, inc=1, device_id={"narrow": other}, device_id_type=MESH)

    own_rows = pl.ds(pl.multiple_of(gather.me * shard_rows, 16), shard_rows)
    load_qkv = pltpu.make_async_copy(w_qkv, qkv_rows.at[own_rows, :], local_sem.at[0])
    load_out = pltpu.make_async_copy(w_out, out_rows.at[own_rows, :], local_sem.at[1])
    load_hidden = pltpu.make_async_copy(hidden, inputs.at[column], local_sem.at[2])
    load_cache = pltpu.make_async_copy(cache, cache_here, local_sem.at[3])
    load_scales = pltpu.make_async_copy(scales, scales_all.at[column], local_sem.at[4])
    for load in (load_qkv, load_out, load_hidden, load_scales, load_cache):
        load.start()

    has_lower = (gather.z + CHIPS_Z - 1) // CHIPS_Z
    has_upper = (2 * CHIPS_Z - 2 - gather.z) // CHIPS_Z
    pl.semaphore_wait(barrier, 3 + has_lower + has_upper)

    def beside(source, target, number):
        return pltpu.make_async_remote_copy(
            src_ref=source,
            dst_ref=target,
            send_sem=side_send.at[number],
            recv_sem=side_recv.at[number],
            device_id={"narrow": other},
            device_id_type=MESH,
        )

    load_qkv.wait()
    gather.begin(QKV)
    load_hidden.wait()
    load_scales.wait()
    send_hidden = beside(inputs.at[column], inputs.at[column], 0)
    send_scales = beside(scales_all.at[column], scales_all.at[column], 1)
    send_hidden.start()
    send_scales.start()
    load_out.wait()
    sides = [send_hidden, send_scales]

    block_start = gather.me * cache_count
    rows_global = block_start + lax.broadcasted_iota(jnp.int32, (8, cache_count), 1)
    for request in range(requests):
        start = offsets[request]
        stop = start + lengths[request]
        alive = jnp.logical_and(rows_global >= start, rows_global < stop)
        live[request] = jnp.where(alive, 0.0, NEGATIVE)
    later = lax.broadcasted_iota(jnp.int32, (SPAN, SPAN), 0) < lax.broadcasted_iota(
        jnp.int32, (SPAN, SPAN), 1
    )
    scale_factor = 1.0 / math.sqrt(HEAD)

    for distance in range(CHIPS_Z):
        gather.step(QKV, distance)
    gather.begin(OUT)
    gather.step(QKV, CHIPS_Z)
    gather.finish(QKV)
    send_hidden.wait_recv()
    send_scales.wait_recv()
    load_cache.wait()

    tile = 512

    def project(layer, source):
        def one(j, carry):
            columns = pl.ds(pl.multiple_of(j * tile, tile), tile)
            total = jnp.dot(
                source[0], qkv_rows[:width, columns], preferred_element_type=jnp.float32
            )
            total += jnp.dot(
                source[1], qkv_rows[width:, columns], preferred_element_type=jnp.float32
            )
            projected[layer, :, columns] = (total + qkv_bias[:, columns]).astype(jnp.bfloat16)
            return carry

        lax.fori_loop(0, 3 * width // tile, one, 0)
        stores = []
        for kind in range(2):
            block = projected.at[layer, :, (kind + 1) * width : (kind + 2) * width]
            store = pltpu.make_async_copy(
                block, new_cache.at[layer, kind], local_sem.at[5 + 2 * layer + kind]
            )
            store.start()
            stores.append(store)
        return stores

    def attend_heads(layer, first, count):
        def one(head, carry):
            place = head * HEAD
            here = pl.ds(pl.multiple_of(place, HEAD), HEAD)
            key_columns = pl.ds(pl.multiple_of(place + width, HEAD), HEAD)
            value_columns = pl.ds(pl.multiple_of(place + 2 * width, HEAD), HEAD)
            keys_cached = cache_here[layer, 0, :, here]
            values_cached = cache_here[layer, 1, :, here]
            for request in range(requests):
                rows = slice(request * SPAN, (request + 1) * SPAN)
                queries = projected[layer, rows, here]
                keys_new = projected[layer, rows, key_columns]
                values_new = projected[layer, rows, value_columns]
                contract = (((1,), (1,)), ((), ()))
                scores_cache = lax.dot_general(
                    queries, keys_cached, contract, preferred_element_type=jnp.float32
                )
                scores_new = lax.dot_general(
                    queries, keys_new, contract, preferred_element_type=jnp.float32
                )
                scores_cache = scores_cache * scale_factor + live[request, 0:1, :]
                scores_new = jnp.where(later, NEGATIVE, scores_new * scale_factor)
                top = jnp.maximum(
                    jnp.max(scores_cache, axis=1, keepdims=True),
                    jnp.max(scores_new, axis=1, keepdims=True),
                )
                weights_cache = jnp.exp(scores_cache - top)
                weights_new = jnp.exp(scores_new - top)
                totals = jnp.sum(weights_cache, axis=1, keepdims=True) + jnp.sum(
                    weights_new, axis=1, keepdims=True
                )
                combined = jnp.dot(
                    weights_cache.astype(jnp.bfloat16),
                    values_cached,
                    preferred_element_type=jnp.float32,
                )
                combined += jnp.dot(
                    weights_new.astype(jnp.bfloat16),
                    values_new,
                    preferred_element_type=jnp.float32,
                )
                attended[layer, column, rows, here] = (combined / totals).astype(jnp.bfloat16)
            return carry

        lax.fori_loop(first, first + count, one, 0)

    group = 2

    def attend_all(layer, between):
        copies = []
        for number, first in enumerate(range(0, heads, group)):
            attend_heads(layer, first, group)
            block = attended.at[layer, column, :, first * HEAD : (first + group) * HEAD]
            copy = beside(block, block, 2 + layer * 4 + number)
            copy.start()
            copies.append(copy)
            between(number)
        return copies

    def mix(layer, carried, after):
        for number in range(width // tile):
            columns = slice(number * tile, (number + 1) * tile)
            total = jnp.dot(
                attended[layer, 0], out_rows[:width, columns], preferred_element_type=jnp.float32
            )
            total += jnp.dot(
                attended[layer, 1], out_rows[width:, columns], preferred_element_type=jnp.float32
            )
            total = total + out_bias[:, columns] + carried[column, :, columns].astype(jnp.float32)
            summed[layer, column, :, columns] = total.astype(jnp.bfloat16)
            after(number, columns)

    stores = project(0, inputs)
    gather.step(OUT, 0)

    def advance(number):
        gather.step(OUT, number + 1)

    copies = attend_all(0, advance)
    gather.finish(OUT)
    for copy in copies:
        copy.wait_recv()
    sides += copies

    exchanged = []

    def share(number, columns):
        block = summed.at[0, column, :, columns]
        copy = beside(block, block, 10 + number)
        copy.start()
        exchanged.append(copy)

    mix(0, inputs, share)
    for copy in exchanged:
        copy.wait_recv()
    sides += exchanged

    chunk = 64

    def norm_rows(j, carry):
        rows = pl.ds(pl.multiple_of(j * chunk, chunk), chunk)
        values = [summed[0, half, rows, :].astype(jnp.float32) for half in range(2)]
        means = sum(jnp.sum(v, axis=1, keepdims=True) for v in values) / full_width
        centered = [v - means for v in values]
        spread = sum(jnp.sum(c * c, axis=1, keepdims=True) for c in centered) / full_width
        inverse = lax.rsqrt(spread + EPSILON)
        for half in range(2):
            scaled = centered[half] * inverse
            scaled = scaled * scales_all[half, 0:1, :] + scales_all[half, 1:2, :]
            normed[half, rows, :] = scaled.astype(jnp.bfloat16)
        return carry

    lax.fori_loop(0, tokens // chunk, norm_rows, 0)

    stores += project(1, normed)
    copies = attend_all(1, lambda number: None)
    for copy in copies:
        copy.wait_recv()
    sides += copies
    mix(1, normed, lambda number, columns: None)

    lane = lax.broadcasted_iota(jnp.int32, (chunk, 128), 1)

    def stat_rows(j, carry):
        rows = pl.ds(pl.multiple_of(j * chunk, chunk), chunk)
        values = summed[1, column, rows, :].astype(jnp.float32)
        mean = jnp.sum(values, axis=1, keepdims=True) / width
        centered = values - mean
        spread = jnp.sum(centered * centered, axis=1, keepdims=True)
        stats[column, rows, :] = jnp.where(lane == 0, mean, jnp.where(lane == 1, spread, 0.0))
        return carry

    lax.fori_loop(0, tokens // chunk, stat_rows, 0)
    send_stats = beside(stats.at[column], stats.at[column], 12)
    send_stats.start()
    send_stats.wait_recv()
    sides.append(send_stats)

    def last_rows(j, carry):
        rows = pl.ds(pl.multiple_of(j * chunk, chunk), chunk)
        mean_a, mean_b = stats[0, rows, 0:1], stats[1, rows, 0:1]
        means = (mean_a + mean_b) * 0.5
        gap = mean_a - mean_b
        spread = stats[0, rows, 1:2] + stats[1, rows, 1:2] + gap * gap * (width * 0.5)
        inverse = lax.rsqrt(spread / full_width + EPSILON)
        scaled = (summed[1, column, rows, :].astype(jnp.float32) - means) * inverse
        scaled = scaled * scales_all[column, 0:1, :] + scales_all[column, 1:2, :]
        hidden_out[rows, :] = scaled.astype(jnp.bfloat16)
        return carry

    lax.fori_loop(0, tokens // chunk, last_rows, 0)

    for store in stores:
        store.wait()
    for copy in sides:
        copy.wait_send()
    gather.drain()


def fused(
    hidden_in,
    cache_lengths,
    cache_offsets,
    cache_kv,
    w_qkv,
    qkv_bias,
    w_out,
    out_bias,
    norm_gain,
    norm_shift,
):
    tokens, width = hidden_in.shape
    cache_count = cache_kv.shape[2]
    shard_rows = w_qkv.shape[0]
    depth = shard_rows * lax.axis_size("wide")
    requests = cache_lengths.shape[0]
    scales = jnp.stack([norm_gain, norm_shift]).astype(jnp.float32)
    scales = jnp.concatenate([scales, jnp.zeros((6, width), jnp.float32)])
    smem = pl.BlockSpec(memory_space=pltpu.SMEM)
    vmem = pl.BlockSpec(memory_space=pltpu.VMEM)
    anywhere = pl.BlockSpec(memory_space=pl.ANY)
    bf16 = jnp.bfloat16
    return pl.pallas_call(
        fused_kernel,
        out_shape=(
            jax.ShapeDtypeStruct((tokens, width), bf16),
            jax.ShapeDtypeStruct((LAYERS, 2, tokens, width), bf16),
        ),
        in_specs=[smem, smem, anywhere, anywhere, anywhere, anywhere, vmem, vmem, anywhere],
        out_specs=(vmem, anywhere),
        scratch_shapes=[
            pltpu.VMEM((depth, 3 * width), bf16),
            pltpu.VMEM((depth, width), bf16),
            pltpu.VMEM((LAYERS, 2, cache_count, width), bf16),
            pltpu.VMEM((2, tokens, width), bf16),
            pltpu.VMEM((LAYERS, tokens, 3 * width), bf16),
            pltpu.VMEM((LAYERS, 2, tokens, width), bf16),
            pltpu.VMEM((LAYERS, 2, tokens, width), bf16),
            pltpu.VMEM((2, tokens, width), bf16),
            pltpu.VMEM((2, 8, width), jnp.float32),
            pltpu.VMEM((2, tokens, 128), jnp.float32),
            pltpu.VMEM((requests, 8, cache_count), jnp.float32),
            pltpu.SemaphoreType.DMA((2, 2, CHIPS_Z * CHIPS_Y, 4)),
            pltpu.SemaphoreType.DMA((2, 2, CHIPS_Z * CHIPS_Y * CORES)),
            pltpu.SemaphoreType.DMA((9,)),
            pltpu.SemaphoreType.DMA((13,)),
            pltpu.SemaphoreType.DMA((13,)),
        ],
        compiler_params=pltpu.CompilerParams(
            collective_id=0, has_side_effects=True, vmem_limit_bytes=VMEM_BYTES
        ),
        cost_estimate=pl.CostEstimate(
            flops=2 * LAYERS * tokens * depth * 4 * width,
            bytes_accessed=2 * depth * 4 * width,
            transcendentals=LAYERS * tokens * cache_count * (width // HEAD),
        ),
    )(
        cache_lengths,
        cache_offsets,
        hidden_in,
        cache_kv,
        w_qkv.reshape(shard_rows, 3 * width),
        w_out,
        qkv_bias.astype(jnp.float32).reshape(1, 3 * width),
        out_bias.astype(jnp.float32).reshape(1, width),
        scales,
    )


def solution(mesh):
    in_specs = (
        P("wide", "narrow"),
        P("wide"),
        P("wide"),
        P(None, None, "wide", "narrow"),
        P("wide", None, "narrow"),
        P(None, "narrow"),
        P("wide", "narrow"),
        P("narrow"),
        P("narrow"),
        P("narrow"),
    )
    out_specs = (P("wide", "narrow"), P(None, None, "wide", "narrow"))
    body = fused if fits_fused(mesh) else shards
    return jax.shard_map(body, mesh=mesh, in_specs=in_specs, out_specs=out_specs, check_vma=False)
```

```python
import functools
import math

import jax
import jax.numpy as jnp
from jax import lax
from jax.experimental import pallas as pl
from jax.experimental.pallas import tpu as pltpu
from jax.sharding import PartitionSpec as P

HEAD = 128
SPAN = 128
LAYERS = 2


EPSILON = 1e-05
NEGATIVE = -1e30


def add_rows(shard_piece, operand):
    piece_rows = shard_piece.shape[0]
    return jnp.dot(operand, shard_piece.reshape(piece_rows, -1), preferred_element_type=jnp.float32)


def norm_slice(summed, norm_gain, norm_shift, full_width):
    values = summed.astype(jnp.float32)
    row_means = lax.psum(jnp.sum(values, axis=1), "narrow") / full_width
    centered = values - row_means[:, None]
    row_spread = lax.psum(jnp.sum(centered * centered, axis=1), "narrow") / full_width
    scaled = centered * lax.rsqrt(row_spread[:, None] + EPSILON)
    return (scaled * norm_gain.astype(jnp.float32) + norm_shift.astype(jnp.float32)).astype(
        jnp.bfloat16
    )


def attend(queries, keys_new, values_new, keys_cache, values_cache, live_cache, live_new):
    scale_factor = 1.0 / math.sqrt(queries.shape[2])
    scores_cache = (
        jnp.einsum("qhd,khd->hqk", queries, keys_cache, preferred_element_type=jnp.float32)
        * scale_factor
    )
    scores_new = (
        jnp.einsum("qhd,khd->hqk", queries, keys_new, preferred_element_type=jnp.float32)
        * scale_factor
    )
    masked_cache = jnp.where(live_cache[None], scores_cache, NEGATIVE)
    masked_new = jnp.where(live_new[None], scores_new, NEGATIVE)
    top_score = jnp.maximum(jnp.max(masked_cache, axis=2), jnp.max(masked_new, axis=2))[:, :, None]
    weights_cache = jnp.where(live_cache[None], jnp.exp(masked_cache - top_score), 0.0)
    weights_new = jnp.where(live_new[None], jnp.exp(masked_new - top_score), 0.0)
    totals = jnp.sum(weights_cache, axis=2, keepdims=True) + jnp.sum(
        weights_new, axis=2, keepdims=True
    )
    probs_cache = (weights_cache / totals).astype(jnp.bfloat16)
    probs_new = (weights_new / totals).astype(jnp.bfloat16)
    combined = jnp.einsum(
        "hqk,khd->qhd", probs_cache, values_cache, preferred_element_type=jnp.float32
    )
    combined = combined + jnp.einsum(
        "hqk,khd->qhd", probs_new, values_new, preferred_element_type=jnp.float32
    )
    return combined.astype(jnp.bfloat16).reshape(queries.shape[0], -1)


def shards(
    hidden_in,
    cache_lengths,
    cache_offsets,
    cache_kv,
    w_qkv,
    qkv_bias,
    w_out,
    out_bias,
    norm_gain,
    norm_shift,
):
    row_count, local_width = hidden_in.shape
    full_width = local_width * lax.axis_size("narrow")
    local_heads = local_width // HEAD
    cache_count = cache_kv.shape[2]
    requests_here = cache_lengths.shape[0]
    block_start = lax.axis_index("wide") * cache_count
    rows_global = block_start + jnp.arange(cache_count, dtype=jnp.int32)
    row_start = jnp.broadcast_to(cache_offsets[:, None], (requests_here, SPAN)).reshape(-1)
    row_stop = row_start + jnp.broadcast_to(cache_lengths[:, None], (requests_here, SPAN)).reshape(
        -1
    )
    live_cache = (rows_global[None, :] >= row_start[:, None]) & (
        rows_global[None, :] < row_stop[:, None]
    )
    owner_index = jnp.arange(row_count, dtype=jnp.int32) // SPAN
    position = jnp.arange(row_count, dtype=jnp.int32) % SPAN
    live_new = (owner_index[:, None] == owner_index[None, :]) & (
        position[:, None] >= position[None, :]
    )
    bias_flat = qkv_bias.astype(jnp.float32).reshape(-1)
    gathered = lax.all_gather(hidden_in, "narrow", axis=1, tiled=True)
    carried = hidden_in
    appended = []
    for layer_index in range(LAYERS):
        projections = add_rows(lax.all_gather(w_qkv, "wide", axis=0, tiled=True), operand=gathered)
        projections = projections + bias_flat
        queries = projections[:, :local_width].astype(jnp.bfloat16)
        keys_new = projections[:, local_width : 2 * local_width].astype(jnp.bfloat16)
        values_new = projections[:, 2 * local_width :].astype(jnp.bfloat16)
        appended.append(jnp.stack([keys_new, values_new]))
        keys_cache = cache_kv[layer_index, 0].reshape(cache_count, local_heads, HEAD)
        values_cache = cache_kv[layer_index, 1].reshape(cache_count, local_heads, HEAD)
        attended = attend(
            queries.reshape(row_count, local_heads, HEAD),
            keys_new.reshape(row_count, local_heads, HEAD),
            values_new.reshape(row_count, local_heads, HEAD),
            keys_cache,
            values_cache,
            live_cache,
            live_new,
        )
        heads_all = lax.all_gather(attended, "narrow", axis=1, tiled=True)
        projected = add_rows(lax.all_gather(w_out, "wide", axis=0, tiled=True), operand=heads_all)
        summed = (projected + out_bias.astype(jnp.float32) + carried.astype(jnp.float32)).astype(
            jnp.bfloat16
        )
        if layer_index + 1 < LAYERS:
            carried = norm_slice(summed, norm_gain, norm_shift, full_width)
            gathered = lax.all_gather(carried, "narrow", axis=1, tiled=True)
        else:
            carried = norm_slice(summed, norm_gain, norm_shift, full_width)
    return (carried, jnp.stack(appended))


MESH = pl.DeviceIdType.MESH
CHIPS_Y = 2
CHIPS_Z = 4
CORES = 2
UP, DOWN, ACROSS, SIBLING = range(4)
QUERY, KEY, VALUE, OUT = range(4)
QKV = (QUERY, KEY, VALUE)
FIRST, SECOND = range(2)
VMEM_BYTES = 48 * 1024 * 1024


def fits_fused(mesh):
    return mesh.shape["wide"] == CHIPS_Z * CHIPS_Y * CORES and mesh.shape["narrow"] == 2


class Gather:
    def __init__(self, buffers, shard_rows, cuts, send_sem, recv_sem):
        self.buffers, self.shard_rows, self.cuts = buffers, shard_rows, cuts
        self.send_sem, self.recv_sem = send_sem, recv_sem
        me = lax.axis_index("wide")
        self.core = lax.rem(me, CORES)
        self.y = lax.rem(me // CORES, CHIPS_Y)
        self.z = me // (CORES * CHIPS_Y)
        self.me = me
        self.targets = {
            UP: (self.z + 1 < CHIPS_Z, me + CORES * CHIPS_Y),
            DOWN: (self.z > 0, me - CORES * CHIPS_Y),
            ACROSS: (True, self.index(self.z, 1 - self.y, self.core)),
            SIBLING: (True, self.index(self.z, self.y, 1 - self.core)),
        }
        self.pending = []

    def index(self, z, y, core):
        return (z * CHIPS_Y + y) * CORES + core

    def slot(self, which, part, source):
        cut = self.cuts[which]
        start = source * self.shard_rows + (0 if part == FIRST else cut)
        size = cut if part == FIRST else self.shard_rows - cut
        buffer, columns = self.buffers[which]
        return buffer.at[pl.ds(pl.multiple_of(start, 16), size), columns]

    def copy(self, which, part, z, y, core, kind):
        source = self.index(z, y, core)
        block = self.slot(which, part, source)
        return pltpu.make_async_remote_copy(
            src_ref=block,
            dst_ref=block,
            send_sem=self.send_sem.at[which, part, z * CHIPS_Y + y, kind],
            recv_sem=self.recv_sem.at[which, part, source],
            device_id={"wide": self.targets[kind][1]},
            device_id_type=MESH,
        )

    def send(self, which, part, z, y, kinds, valid=True):
        for kind in kinds:
            condition = self.targets[kind][0]
            if condition is True:
                condition = valid
            elif valid is not True:
                condition = jnp.logical_and(condition, valid)
            make = functools.partial(self.copy, which, part, z, y, self.core, kind)
            self.when(condition, lambda make=make: make().start())
            self.pending.append((condition, make))

    def when(self, condition, action):
        if condition is True:
            action()
        else:
            pl.when(condition)(action)

    def arrive(self, which, part, z, y, core, valid=True):
        make = functools.partial(self.copy, which, part, z, y, core, SIBLING)
        self.when(valid, lambda: make().wait_recv())

    def begin(self, which):
        z, y = self.z, self.y
        self.send(which, SECOND, z, y, (ACROSS,))
        self.send(which, FIRST, z, y, (UP, DOWN, ACROSS))
        self.send(which, SECOND, z, y, (UP, DOWN))
        self.send(which, FIRST, z, y, (SIBLING,))
        self.send(which, SECOND, z, y, (SIBLING,))

    def around(self, distance):
        low, high = self.z - distance, self.z + distance
        return ((low, low >= 0, UP), (high, high < CHIPS_Z, DOWN))

    def take_across(self, which, distance):
        y = 1 - self.y
        places = ((self.z, True, None),) if distance == 0 else self.around(distance)
        for z, valid, _ in places:
            self.arrive(which, FIRST, z, y, self.core, valid)
            self.send(which, FIRST, z, y, (SIBLING,), valid)

    def step(self, which, distance):
        if distance == 0:
            y = 1 - self.y
            self.arrive(which, SECOND, self.z, y, self.core)
            self.send(which, SECOND, self.z, y, (UP, DOWN, SIBLING))
            return
        if distance < CHIPS_Z:
            for z, valid, onward in self.around(distance):
                self.arrive(which, FIRST, z, self.y, self.core, valid)
                self.send(which, FIRST, z, self.y, (onward, ACROSS, SIBLING), valid)
            for z, valid, onward in self.around(distance):
                for y in (self.y, 1 - self.y):
                    self.arrive(which, SECOND, z, y, self.core, valid)
                    self.send(which, SECOND, z, y, (onward, SIBLING), valid)
        self.take_across(which, distance - 1)

    def finish(self, which):
        for part in (FIRST, SECOND):
            for z in range(CHIPS_Z):
                for y in range(CHIPS_Y):
                    self.arrive(which, part, z, y, 1 - self.core)

    def drain(self):
        for condition, make in self.pending:
            self.when(condition, lambda make=make: make().wait_send())
        self.pending = []


def fused_kernel(
    lengths,
    offsets,
    hidden,
    cache,
    w_qkv,
    w_out,
    qkv_bias,
    out_bias,
    norm_gain,
    norm_shift,
    hidden_out,
    new_cache,
    qkv_rows,
    out_rows,
    cache_here,
    inputs,
    projected,
    attended,
    summed,
    normed,
    scales_all,
    biases,
    stats,
    stats_wide,
    live,
    send_sem,
    recv_sem,
    local_sem,
    side_send,
    side_recv,
):
    tokens, width = hidden.shape
    cache_count = cache.shape[2]
    requests = lengths.shape[0]
    shard_rows = w_out.shape[0]
    heads = width // HEAD
    full_width = 2 * width
    column = lax.axis_index("narrow")
    other = 1 - column
    buffers = [(qkv_rows, slice(kind * width, (kind + 1) * width)) for kind in QKV]
    buffers.append((out_rows, slice(0, width)))
    gather = Gather(buffers, shard_rows, (112, 112, 112, 96), send_sem, recv_sem)

    barrier = pltpu.get_barrier_semaphore()
    for condition, target in gather.targets.values():

        def greet(target=target):
            pl.semaphore_signal(
                barrier, inc=1, device_id={"wide": target}, device_id_type=MESH
            )

        gather.when(condition, greet)
    pl.semaphore_signal(barrier, inc=1, device_id={"narrow": other}, device_id_type=MESH)

    own_rows = pl.ds(pl.multiple_of(gather.me * shard_rows, 16), shard_rows)
    load_qkv = [
        pltpu.make_async_copy(
            w_qkv.at[kind], qkv_rows.at[own_rows, buffers[kind][1]], local_sem.at[9 + kind]
        )
        for kind in QKV
    ]
    load_out = pltpu.make_async_copy(w_out, out_rows.at[own_rows, :], local_sem.at[1])
    load_hidden = pltpu.make_async_copy(hidden, inputs.at[column], local_sem.at[2])
    load_cache = pltpu.make_async_copy(cache, cache_here, local_sem.at[3])
    for load in (*load_qkv, load_hidden, load_out, load_cache):
        load.start()

    has_lower = (gather.z + CHIPS_Z - 1) // CHIPS_Z
    has_upper = (2 * CHIPS_Z - 2 - gather.z) // CHIPS_Z
    pl.semaphore_wait(barrier, 3 + has_lower + has_upper)

    def beside(source, target, number):
        return pltpu.make_async_remote_copy(
            src_ref=source,
            dst_ref=target,
            send_sem=side_send.at[number],
            recv_sem=side_recv.at[number],
            device_id={"narrow": other},
            device_id_type=MESH,
        )

    for kind in QKV:
        load_qkv[kind].wait()
        gather.begin(kind)
    load_hidden.wait()
    scales_all[column, 0:1, :] = norm_gain[...].astype(jnp.float32).reshape(1, width)
    scales_all[column, 1:2, :] = norm_shift[...].astype(jnp.float32).reshape(1, width)
    scales_all[column, 2:8, :] = jnp.zeros((6, width), jnp.float32)
    biases[0:1, :] = out_bias[...].astype(jnp.float32).reshape(1, width)
    for kind in QKV:
        biases[kind + 1 : kind + 2, :] = qkv_bias[kind : kind + 1, :].astype(jnp.float32)
    send_hidden = beside(inputs.at[column], inputs.at[column], 0)
    send_scales = beside(scales_all.at[column], scales_all.at[column], 1)
    send_hidden.start()
    send_scales.start()
    load_out.wait()
    sides = [send_hidden, send_scales]

    block_start = gather.me * cache_count
    rows_global = block_start + lax.broadcasted_iota(jnp.int32, (8, cache_count), 1)
    for request in range(requests):
        start = offsets[request]
        stop = start + lengths[request]
        alive = jnp.logical_and(rows_global >= start, rows_global < stop)
        live[request] = jnp.where(alive, 0.0, NEGATIVE)
    later = lax.broadcasted_iota(jnp.int32, (SPAN, SPAN), 0) < lax.broadcasted_iota(
        jnp.int32, (SPAN, SPAN), 1
    )
    scale_factor = 1.0 / math.sqrt(HEAD)

    for distance in range(CHIPS_Z):
        for kind in QKV:
            gather.step(kind, distance)
    gather.begin(OUT)
    for kind in QKV:
        gather.step(kind, CHIPS_Z)
    gather.step(OUT, 0)
    gather.step(OUT, 1)
    for kind in QKV:
        gather.finish(kind)
    send_hidden.wait_recv()
    send_scales.wait_recv()
    load_cache.wait()

    tile = 512

    def project(layer, source, between):
        for kind in QKV:

            def one(j, carry, kind=kind):
                here = pl.ds(pl.multiple_of(j * tile, tile), tile)
                columns = pl.ds(pl.multiple_of(kind * width + j * tile, tile), tile)
                total = jnp.dot(
                    source[0], qkv_rows[:width, columns], preferred_element_type=jnp.float32
                )
                total += jnp.dot(
                    source[1], qkv_rows[width:, columns], preferred_element_type=jnp.float32
                )
                total = total + biases[kind + 1 : kind + 2, here]
                projected[layer, :, columns] = total.astype(jnp.bfloat16)
                return carry

            lax.fori_loop(0, width // tile, one, 0)
            between(kind)
        stores = []
        for kind in range(2):
            block = projected.at[layer, :, (kind + 1) * width : (kind + 2) * width]
            store = pltpu.make_async_copy(
                block, new_cache.at[layer, kind], local_sem.at[5 + 2 * layer + kind]
            )
            store.start()
            stores.append(store)
        return stores

    contract = (((1,), (1,)), ((), ()))
    exponent_scale = scale_factor * math.log2(math.e)

    def attend_heads(layer, first, count):
        for head in range(first, first + count):
            here = slice(head * HEAD, (head + 1) * HEAD)
            key_columns = slice(width + head * HEAD, width + (head + 1) * HEAD)
            value_columns = slice(2 * width + head * HEAD, 2 * width + (head + 1) * HEAD)
            scores_all = lax.dot_general(
                projected[layer, :, here],
                cache_here[layer, 0, :, here],
                contract,
                preferred_element_type=jnp.float32,
            )
            weights_all, totals, combined_new = [], [], []
            for request in range(requests):
                rows = slice(request * SPAN, (request + 1) * SPAN)
                scores_new = lax.dot_general(
                    projected[layer, rows, here],
                    projected[layer, rows, key_columns],
                    contract,
                    preferred_element_type=jnp.float32,
                )
                scores_cache = scores_all[rows, :] + live[request, 0:1, :]
                scores_new = jnp.where(later, NEGATIVE, scores_new)
                top = jnp.maximum(
                    jnp.max(scores_cache, axis=1, keepdims=True),
                    jnp.max(scores_new, axis=1, keepdims=True),
                )
                weights_cache = jnp.exp2((scores_cache - top) * exponent_scale)
                weights_new = jnp.exp2((scores_new - top) * exponent_scale)
                totals.append(
                    jnp.sum(weights_cache, axis=1, keepdims=True)
                    + jnp.sum(weights_new, axis=1, keepdims=True)
                )
                weights_all.append(weights_cache.astype(jnp.bfloat16))
                combined_new.append(
                    jnp.dot(
                        weights_new.astype(jnp.bfloat16),
                        projected[layer, rows, value_columns],
                        preferred_element_type=jnp.float32,
                    )
                )
            combined = jnp.dot(
                jnp.concatenate(weights_all, axis=0),
                cache_here[layer, 1, :, here],
                preferred_element_type=jnp.float32,
            )
            combined = (combined + jnp.concatenate(combined_new, axis=0)) / jnp.concatenate(
                totals, axis=0
            )
            attended[layer, column, :, here] = combined.astype(jnp.bfloat16)

    group = 2
    mix_tile = 256

    def attend_all(layer, between):
        copies = []
        for number, first in enumerate(range(0, heads, group)):
            attend_heads(layer, first, group)
            block = attended.at[layer, column, :, first * HEAD : (first + group) * HEAD]
            copy = beside(block, block, 2 + layer * 4 + number)
            copy.start()
            copies.append(copy)
            between(number)
        return copies

    def mix(layer, carried, after):
        for number in range(width // mix_tile):
            columns = slice(number * mix_tile, (number + 1) * mix_tile)
            total = jnp.dot(
                attended[layer, 0], out_rows[:width, columns], preferred_element_type=jnp.float32
            )
            total += jnp.dot(
                attended[layer, 1], out_rows[width:, columns], preferred_element_type=jnp.float32
            )
            total = total + biases[0:1, columns] + carried[column, :, columns].astype(jnp.float32)
            summed[layer, column, :, columns] = total.astype(jnp.bfloat16)
            after(number, columns)

    def advance_early(kind):
        if kind == KEY:
            gather.step(OUT, 2)

    def advance(number):
        if number == 0:
            gather.step(OUT, 3)
        if number == 2:
            gather.step(OUT, 4)

    stores = project(0, inputs, advance_early)
    copies = attend_all(0, advance)
    gather.drain()
    gather.finish(OUT)
    for copy in copies:
        copy.wait_recv()
    sides += copies

    exchanged = []

    def share(number, columns):
        block = summed.at[0, column, :, columns]
        copy = beside(block, block, 10 + number)
        copy.start()
        exchanged.append(copy)

    mix(0, inputs, share)
    for copy in exchanged:
        copy.wait_recv()
    sides += exchanged

    chunk = 64

    def norm_rows(j, carry):
        rows = pl.ds(pl.multiple_of(j * chunk, chunk), chunk)
        values = [summed[0, half, rows, :].astype(jnp.float32) for half in range(2)]
        means = sum(jnp.sum(v, axis=1, keepdims=True) for v in values) / full_width
        centered = [v - means for v in values]
        spread = sum(jnp.sum(c * c, axis=1, keepdims=True) for c in centered) / full_width
        inverse = lax.rsqrt(spread + EPSILON)
        for half in range(2):
            scaled = centered[half] * inverse
            scaled = scaled * scales_all[half, 0:1, :] + scales_all[half, 1:2, :]
            normed[half, rows, :] = scaled.astype(jnp.bfloat16)
        return carry

    lax.fori_loop(0, tokens // chunk, norm_rows, 0)

    stores += project(1, normed, lambda kind: None)
    copies = attend_all(1, lambda number: None)
    for copy in copies:
        copy.wait_recv()
    sides += copies
    mix(1, normed, lambda number, columns: None)

    lane = lax.broadcasted_iota(jnp.int32, (chunk, 128), 1)

    def stat_rows(j, carry):
        rows = pl.ds(pl.multiple_of(j * chunk, chunk), chunk)
        values = summed[1, column, rows, :].astype(jnp.float32)
        mean = jnp.sum(values, axis=1, keepdims=True) / width
        centered = values - mean
        spread = jnp.sum(centered * centered, axis=1, keepdims=True)
        stats_wide[0, rows, :] = jnp.where(lane == 0, mean, jnp.where(lane == 1, spread, 0.0))
        return carry

    lax.fori_loop(0, tokens // chunk, stat_rows, 0)
    stats[column] = jnp.transpose(stats_wide[0])[:8, :]
    send_stats = beside(stats.at[column], stats.at[column], 14)
    send_stats.start()
    send_stats.wait_recv()
    sides.append(send_stats)
    for half in range(2):
        padded = jnp.concatenate([stats[half], jnp.zeros((120, tokens), jnp.float32)], axis=0)
        stats_wide[half] = jnp.transpose(padded)

    def last_rows(j, carry):
        rows = pl.ds(pl.multiple_of(j * chunk, chunk), chunk)
        mean_a, mean_b = stats_wide[0, rows, 0:1], stats_wide[1, rows, 0:1]
        means = (mean_a + mean_b) * 0.5
        gap = mean_a - mean_b
        spread = stats_wide[0, rows, 1:2] + stats_wide[1, rows, 1:2] + gap * gap * (width * 0.5)
        inverse = lax.rsqrt(spread / full_width + EPSILON)
        scaled = (summed[1, column, rows, :].astype(jnp.float32) - means) * inverse
        scaled = scaled * scales_all[column, 0:1, :] + scales_all[column, 1:2, :]
        hidden_out[rows, :] = scaled.astype(jnp.bfloat16)
        return carry

    lax.fori_loop(0, tokens // chunk, last_rows, 0)

    for store in stores:
        store.wait()
    for copy in sides:
        copy.wait_send()


def fused(
    hidden_in,
    cache_lengths,
    cache_offsets,
    cache_kv,
    w_qkv,
    qkv_bias,
    w_out,
    out_bias,
    norm_gain,
    norm_shift,
):
    tokens, width = hidden_in.shape
    cache_count = cache_kv.shape[2]
    shard_rows = w_qkv.shape[0]
    depth = shard_rows * lax.axis_size("wide")
    requests = cache_lengths.shape[0]
    smem = pl.BlockSpec(memory_space=pltpu.SMEM)
    vmem = pl.BlockSpec(memory_space=pltpu.VMEM)
    anywhere = pl.BlockSpec(memory_space=pl.ANY)
    bf16 = jnp.bfloat16
    return pl.pallas_call(
        fused_kernel,
        out_shape=(
            jax.ShapeDtypeStruct((tokens, width), bf16),
            jax.ShapeDtypeStruct((LAYERS, 2, tokens, width), bf16),
        ),
        in_specs=[smem, smem, anywhere, anywhere, anywhere, anywhere, vmem, vmem, vmem, vmem],
        out_specs=(vmem, anywhere),
        scratch_shapes=[
            pltpu.VMEM((depth, 3 * width), bf16),
            pltpu.VMEM((depth, width), bf16),
            pltpu.VMEM((LAYERS, 2, cache_count, width), bf16),
            pltpu.VMEM((2, tokens, width), bf16),
            pltpu.VMEM((LAYERS, tokens, 3 * width), bf16),
            pltpu.VMEM((LAYERS, 2, tokens, width), bf16),
            pltpu.VMEM((LAYERS, 2, tokens, width), bf16),
            pltpu.VMEM((2, tokens, width), bf16),
            pltpu.VMEM((2, 8, width), jnp.float32),
            pltpu.VMEM((8, width), jnp.float32),
            pltpu.VMEM((2, 8, tokens), jnp.float32),
            pltpu.VMEM((2, tokens, 128), jnp.float32),
            pltpu.VMEM((requests, 8, cache_count), jnp.float32),
            pltpu.SemaphoreType.DMA((4, 2, CHIPS_Z * CHIPS_Y, 4)),
            pltpu.SemaphoreType.DMA((4, 2, CHIPS_Z * CHIPS_Y * CORES)),
            pltpu.SemaphoreType.DMA((12,)),
            pltpu.SemaphoreType.DMA((15,)),
            pltpu.SemaphoreType.DMA((15,)),
        ],
        compiler_params=pltpu.CompilerParams(
            collective_id=0, has_side_effects=True, vmem_limit_bytes=VMEM_BYTES
        ),
        cost_estimate=pl.CostEstimate(
            flops=2 * LAYERS * tokens * depth * 4 * width,
            bytes_accessed=2 * depth * 4 * width,
            transcendentals=LAYERS * tokens * cache_count * (width // HEAD),
        ),
    )(
        cache_lengths,
        cache_offsets,
        hidden_in,
        cache_kv,
        jnp.transpose(w_qkv, (1, 0, 2)),
        w_out,
        qkv_bias,
        out_bias,
        norm_gain,
        norm_shift,
    )


def solution(mesh):
    in_specs = (
        P("wide", "narrow"),
        P("wide"),
        P("wide"),
        P(None, None, "wide", "narrow"),
        P("wide", None, "narrow"),
        P(None, "narrow"),
        P("wide", "narrow"),
        P("narrow"),
        P("narrow"),
        P("narrow"),
    )
    out_specs = (P("wide", "narrow"), P(None, None, "wide", "narrow"))
    body = fused if fits_fused(mesh) else shards
    return jax.shard_map(body, mesh=mesh, in_specs=in_specs, out_specs=out_specs, check_vma=False)
```

```python
import functools
import math

import jax
import jax.numpy as jnp
from jax import lax
from jax.experimental import pallas as pl
from jax.experimental.pallas import tpu as pltpu
from jax.sharding import PartitionSpec as P

HEAD = 128
SPAN = 128
LAYERS = 2


EPSILON = 1e-05
NEGATIVE = -1e30


def add_rows(shard_piece, operand):
    piece_rows = shard_piece.shape[0]
    return jnp.dot(operand, shard_piece.reshape(piece_rows, -1), preferred_element_type=jnp.float32)


def norm_slice(summed, norm_gain, norm_shift, full_width):
    values = summed.astype(jnp.float32)
    row_means = lax.psum(jnp.sum(values, axis=1), "narrow") / full_width
    centered = values - row_means[:, None]
    row_spread = lax.psum(jnp.sum(centered * centered, axis=1), "narrow") / full_width
    scaled = centered * lax.rsqrt(row_spread[:, None] + EPSILON)
    return (scaled * norm_gain.astype(jnp.float32) + norm_shift.astype(jnp.float32)).astype(
        jnp.bfloat16
    )


def attend(queries, keys_new, values_new, keys_cache, values_cache, live_cache, live_new):
    scale_factor = 1.0 / math.sqrt(queries.shape[2])
    scores_cache = (
        jnp.einsum("qhd,khd->hqk", queries, keys_cache, preferred_element_type=jnp.float32)
        * scale_factor
    )
    scores_new = (
        jnp.einsum("qhd,khd->hqk", queries, keys_new, preferred_element_type=jnp.float32)
        * scale_factor
    )
    masked_cache = jnp.where(live_cache[None], scores_cache, NEGATIVE)
    masked_new = jnp.where(live_new[None], scores_new, NEGATIVE)
    top_score = jnp.maximum(jnp.max(masked_cache, axis=2), jnp.max(masked_new, axis=2))[:, :, None]
    weights_cache = jnp.where(live_cache[None], jnp.exp(masked_cache - top_score), 0.0)
    weights_new = jnp.where(live_new[None], jnp.exp(masked_new - top_score), 0.0)
    totals = jnp.sum(weights_cache, axis=2, keepdims=True) + jnp.sum(
        weights_new, axis=2, keepdims=True
    )
    probs_cache = (weights_cache / totals).astype(jnp.bfloat16)
    probs_new = (weights_new / totals).astype(jnp.bfloat16)
    combined = jnp.einsum(
        "hqk,khd->qhd", probs_cache, values_cache, preferred_element_type=jnp.float32
    )
    combined = combined + jnp.einsum(
        "hqk,khd->qhd", probs_new, values_new, preferred_element_type=jnp.float32
    )
    return combined.astype(jnp.bfloat16).reshape(queries.shape[0], -1)


def shards(
    hidden_in,
    cache_lengths,
    cache_offsets,
    cache_kv,
    w_qkv,
    qkv_bias,
    w_out,
    out_bias,
    norm_gain,
    norm_shift,
):
    row_count, local_width = hidden_in.shape
    full_width = local_width * lax.axis_size("narrow")
    local_heads = local_width // HEAD
    cache_count = cache_kv.shape[2]
    requests_here = cache_lengths.shape[0]
    block_start = lax.axis_index("wide") * cache_count
    rows_global = block_start + jnp.arange(cache_count, dtype=jnp.int32)
    row_start = jnp.broadcast_to(cache_offsets[:, None], (requests_here, SPAN)).reshape(-1)
    row_stop = row_start + jnp.broadcast_to(cache_lengths[:, None], (requests_here, SPAN)).reshape(
        -1
    )
    live_cache = (rows_global[None, :] >= row_start[:, None]) & (
        rows_global[None, :] < row_stop[:, None]
    )
    owner_index = jnp.arange(row_count, dtype=jnp.int32) // SPAN
    position = jnp.arange(row_count, dtype=jnp.int32) % SPAN
    live_new = (owner_index[:, None] == owner_index[None, :]) & (
        position[:, None] >= position[None, :]
    )
    bias_flat = qkv_bias.astype(jnp.float32).reshape(-1)
    gathered = lax.all_gather(hidden_in, "narrow", axis=1, tiled=True)
    carried = hidden_in
    appended = []
    for layer_index in range(LAYERS):
        projections = add_rows(lax.all_gather(w_qkv, "wide", axis=0, tiled=True), operand=gathered)
        projections = projections + bias_flat
        queries = projections[:, :local_width].astype(jnp.bfloat16)
        keys_new = projections[:, local_width : 2 * local_width].astype(jnp.bfloat16)
        values_new = projections[:, 2 * local_width :].astype(jnp.bfloat16)
        appended.append(jnp.stack([keys_new, values_new]))
        keys_cache = cache_kv[layer_index, 0].reshape(cache_count, local_heads, HEAD)
        values_cache = cache_kv[layer_index, 1].reshape(cache_count, local_heads, HEAD)
        attended = attend(
            queries.reshape(row_count, local_heads, HEAD),
            keys_new.reshape(row_count, local_heads, HEAD),
            values_new.reshape(row_count, local_heads, HEAD),
            keys_cache,
            values_cache,
            live_cache,
            live_new,
        )
        heads_all = lax.all_gather(attended, "narrow", axis=1, tiled=True)
        projected = add_rows(lax.all_gather(w_out, "wide", axis=0, tiled=True), operand=heads_all)
        summed = (projected + out_bias.astype(jnp.float32) + carried.astype(jnp.float32)).astype(
            jnp.bfloat16
        )
        if layer_index + 1 < LAYERS:
            carried = norm_slice(summed, norm_gain, norm_shift, full_width)
            gathered = lax.all_gather(carried, "narrow", axis=1, tiled=True)
        else:
            carried = norm_slice(summed, norm_gain, norm_shift, full_width)
    return (carried, jnp.stack(appended))


MESH = pl.DeviceIdType.MESH
CHIPS_Y = 2
CHIPS_Z = 4
CORES = 2
UP, DOWN, ACROSS, SIBLING = range(4)
QUERY, KEY, VALUE, OUT = range(4)
QKV = (QUERY, KEY, VALUE)
FIRST, SECOND = range(2)
VMEM_BYTES = 48 * 1024 * 1024


def fits_fused(mesh):
    return mesh.shape["wide"] == CHIPS_Z * CHIPS_Y * CORES and mesh.shape["narrow"] == 2


class Gather:
    def __init__(self, buffers, shard_rows, cuts, send_sem, recv_sem):
        self.buffers, self.shard_rows, self.cuts = buffers, shard_rows, cuts
        self.send_sem, self.recv_sem = send_sem, recv_sem
        me = lax.axis_index("wide")
        self.core = lax.rem(me, CORES)
        self.y = lax.rem(me // CORES, CHIPS_Y)
        self.z = me // (CORES * CHIPS_Y)
        self.me = me
        self.targets = {
            UP: (self.z + 1 < CHIPS_Z, me + CORES * CHIPS_Y),
            DOWN: (self.z > 0, me - CORES * CHIPS_Y),
            ACROSS: (True, self.index(self.z, 1 - self.y, self.core)),
            SIBLING: (True, self.index(self.z, self.y, 1 - self.core)),
        }
        self.pending = []

    def index(self, z, y, core):
        return (z * CHIPS_Y + y) * CORES + core

    def slot(self, which, part, source):
        cut = self.cuts[which]
        start = source * self.shard_rows + (0 if part == FIRST else cut)
        size = cut if part == FIRST else self.shard_rows - cut
        buffer, columns = self.buffers[which]
        return buffer.at[pl.ds(pl.multiple_of(start, 16), size), columns]

    def copy(self, which, part, z, y, core, kind):
        source = self.index(z, y, core)
        block = self.slot(which, part, source)
        return pltpu.make_async_remote_copy(
            src_ref=block,
            dst_ref=block,
            send_sem=self.send_sem.at[which, part, z * CHIPS_Y + y, kind],
            recv_sem=self.recv_sem.at[which, part, source],
            device_id={"wide": self.targets[kind][1]},
            device_id_type=MESH,
        )

    def send(self, which, part, z, y, kinds, valid=True):
        for kind in kinds:
            condition = self.targets[kind][0]
            if condition is True:
                condition = valid
            elif valid is not True:
                condition = jnp.logical_and(condition, valid)
            make = functools.partial(self.copy, which, part, z, y, self.core, kind)
            self.when(condition, lambda make=make: make().start())
            self.pending.append((condition, make))

    def when(self, condition, action):
        if condition is True:
            action()
        else:
            pl.when(condition)(action)

    def arrive(self, which, part, z, y, core, valid=True):
        make = functools.partial(self.copy, which, part, z, y, core, SIBLING)
        self.when(valid, lambda: make().wait_recv())

    def begin(self, which):
        z, y = self.z, self.y
        self.send(which, SECOND, z, y, (ACROSS,))
        self.send(which, FIRST, z, y, (UP, DOWN, ACROSS))
        self.send(which, SECOND, z, y, (UP, DOWN))
        self.send(which, FIRST, z, y, (SIBLING,))
        self.send(which, SECOND, z, y, (SIBLING,))

    def around(self, distance):
        low, high = self.z - distance, self.z + distance
        return ((low, low >= 0, UP), (high, high < CHIPS_Z, DOWN))

    def take_across(self, which, distance):
        y = 1 - self.y
        places = ((self.z, True, None),) if distance == 0 else self.around(distance)
        for z, valid, _ in places:
            self.arrive(which, FIRST, z, y, self.core, valid)
            self.send(which, FIRST, z, y, (SIBLING,), valid)

    def step(self, which, distance):
        if distance == 0:
            y = 1 - self.y
            self.arrive(which, SECOND, self.z, y, self.core)
            self.send(which, SECOND, self.z, y, (UP, DOWN, SIBLING))
            return
        if distance < CHIPS_Z:
            for z, valid, onward in self.around(distance):
                self.arrive(which, FIRST, z, self.y, self.core, valid)
                self.send(which, FIRST, z, self.y, (onward, ACROSS, SIBLING), valid)
            for z, valid, onward in self.around(distance):
                for y in (self.y, 1 - self.y):
                    self.arrive(which, SECOND, z, y, self.core, valid)
                    self.send(which, SECOND, z, y, (onward, SIBLING), valid)
        self.take_across(which, distance - 1)

    def finish(self, which):
        for part in (FIRST, SECOND):
            for z in range(CHIPS_Z):
                for y in range(CHIPS_Y):
                    self.arrive(which, part, z, y, 1 - self.core)

    def drain(self):
        for condition, make in self.pending:
            self.when(condition, lambda make=make: make().wait_send())
        self.pending = []


def fused_kernel(
    lengths_in,
    offsets_in,
    hidden,
    cache,
    w_qkv,
    w_out,
    qkv_bias_in,
    out_bias_in,
    norm_gain_in,
    norm_shift_in,
    hidden_out,
    new_cache,
    lengths,
    offsets,
    qkv_bias,
    out_bias,
    norm_gain,
    norm_shift,
    qkv_rows,
    out_rows,
    cache_here,
    inputs,
    projected,
    attended,
    summed,
    normed,
    scales_all,
    biases,
    stats,
    stats_wide,
    live,
    send_sem,
    recv_sem,
    local_sem,
    side_send,
    side_recv,
):
    tokens, width = hidden.shape
    cache_count = cache.shape[2]
    requests = lengths.shape[0]
    shard_rows = w_out.shape[0]
    heads = width // HEAD
    full_width = 2 * width
    column = lax.axis_index("narrow")
    other = 1 - column
    buffers = [(qkv_rows, slice(kind * width, (kind + 1) * width)) for kind in QKV]
    buffers.append((out_rows, slice(0, width)))
    gather = Gather(buffers, shard_rows, (112, 112, 112, 96), send_sem, recv_sem)

    barrier = pltpu.get_barrier_semaphore()
    for condition, target in gather.targets.values():

        def greet(target=target):
            pl.semaphore_signal(
                barrier, inc=1, device_id={"wide": target}, device_id_type=MESH
            )

        gather.when(condition, greet)
    pl.semaphore_signal(barrier, inc=1, device_id={"narrow": other}, device_id_type=MESH)

    own_rows = pl.ds(pl.multiple_of(gather.me * shard_rows, 16), shard_rows)
    load_qkv = [
        pltpu.make_async_copy(
            w_qkv.at[kind], qkv_rows.at[own_rows, buffers[kind][1]], local_sem.at[9 + kind]
        )
        for kind in QKV
    ]
    load_out = pltpu.make_async_copy(w_out, out_rows.at[own_rows, :], local_sem.at[1])
    load_hidden = pltpu.make_async_copy(hidden, inputs.at[column], local_sem.at[2])
    load_cache = pltpu.make_async_copy(cache, cache_here, local_sem.at[3])
    pairs = (
        (lengths_in, lengths),
        (offsets_in, offsets),
        (qkv_bias_in, qkv_bias),
        (out_bias_in, out_bias),
        (norm_gain_in, norm_gain),
        (norm_shift_in, norm_shift),
    )
    load_small = [
        pltpu.make_async_copy(source, target, local_sem.at[12 + number])
        for number, (source, target) in enumerate(pairs)
    ]
    for load in (*load_qkv, load_hidden, load_out, *load_small, load_cache):
        load.start()

    has_lower = (gather.z + CHIPS_Z - 1) // CHIPS_Z
    has_upper = (2 * CHIPS_Z - 2 - gather.z) // CHIPS_Z
    pl.semaphore_wait(barrier, 3 + has_lower + has_upper)

    def beside(source, target, number):
        return pltpu.make_async_remote_copy(
            src_ref=source,
            dst_ref=target,
            send_sem=side_send.at[number],
            recv_sem=side_recv.at[number],
            device_id={"narrow": other},
            device_id_type=MESH,
        )

    for kind in QKV:
        load_qkv[kind].wait()
        gather.begin(kind)
    load_hidden.wait()
    for load in load_small:
        load.wait()
    scales_all[column, 0:1, :] = norm_gain[...].astype(jnp.float32).reshape(1, width)
    scales_all[column, 1:2, :] = norm_shift[...].astype(jnp.float32).reshape(1, width)
    scales_all[column, 2:8, :] = jnp.zeros((6, width), jnp.float32)
    biases[0:1, :] = out_bias[...].astype(jnp.float32).reshape(1, width)
    for kind in QKV:
        biases[kind + 1 : kind + 2, :] = qkv_bias[kind : kind + 1, :].astype(jnp.float32)
    send_hidden = beside(inputs.at[column], inputs.at[column], 0)
    send_scales = beside(scales_all.at[column], scales_all.at[column], 1)
    send_hidden.start()
    send_scales.start()
    load_out.wait()
    sides = [send_hidden, send_scales]

    block_start = gather.me * cache_count
    rows_global = block_start + lax.broadcasted_iota(jnp.int32, (8, cache_count), 1)
    for request in range(requests):
        start = offsets[request]
        stop = start + lengths[request]
        alive = jnp.logical_and(rows_global >= start, rows_global < stop)
        live[request] = jnp.where(alive, 0.0, NEGATIVE)
    later = lax.broadcasted_iota(jnp.int32, (SPAN, SPAN), 0) < lax.broadcasted_iota(
        jnp.int32, (SPAN, SPAN), 1
    )
    scale_factor = 1.0 / math.sqrt(HEAD)

    for distance in range(CHIPS_Z):
        for kind in QKV:
            gather.step(kind, distance)
    gather.begin(OUT)
    for kind in QKV:
        gather.step(kind, CHIPS_Z)
    gather.step(OUT, 0)
    gather.step(OUT, 1)
    for kind in QKV:
        gather.finish(kind)
    send_hidden.wait_recv()
    send_scales.wait_recv()
    load_cache.wait()

    tile = 512

    def project(layer, source, rows, between):
        for kind in QKV:

            def one(j, carry, kind=kind):
                here = pl.ds(pl.multiple_of(j * tile, tile), tile)
                columns = pl.ds(pl.multiple_of(kind * width + j * tile, tile), tile)
                total = jnp.dot(
                    source[0, rows, :], qkv_rows[:width, columns], preferred_element_type=jnp.float32
                )
                total += jnp.dot(
                    source[1, rows, :], qkv_rows[width:, columns], preferred_element_type=jnp.float32
                )
                total = total + biases[kind + 1 : kind + 2, here]
                projected[layer, rows, columns] = total.astype(jnp.bfloat16)
                return carry

            lax.fori_loop(0, width // tile, one, 0)
            between(kind)

    def store_cache(layer):
        stores = []
        for kind in range(2):
            block = projected.at[layer, :, (kind + 1) * width : (kind + 2) * width]
            store = pltpu.make_async_copy(
                block, new_cache.at[layer, kind], local_sem.at[5 + 2 * layer + kind]
            )
            store.start()
            stores.append(store)
        return stores

    contract = (((1,), (1,)), ((), ()))
    exponent_scale = scale_factor * math.log2(math.e)

    def attend_heads(layer, first, count, first_request, last_request):
        span = slice(first_request * SPAN, last_request * SPAN)
        for head in range(first, first + count):
            here = slice(head * HEAD, (head + 1) * HEAD)
            key_columns = slice(width + head * HEAD, width + (head + 1) * HEAD)
            value_columns = slice(2 * width + head * HEAD, 2 * width + (head + 1) * HEAD)
            scores_all = lax.dot_general(
                projected[layer, span, here],
                cache_here[layer, 0, :, here],
                contract,
                preferred_element_type=jnp.float32,
            )
            weights_all, totals, combined_new = [], [], []
            for request in range(first_request, last_request):
                rows = slice(request * SPAN, (request + 1) * SPAN)
                within = request - first_request
                scores_new = lax.dot_general(
                    projected[layer, rows, here],
                    projected[layer, rows, key_columns],
                    contract,
                    preferred_element_type=jnp.float32,
                )
                scores_cache = scores_all[within * SPAN : (within + 1) * SPAN, :] + live[request, 0:1, :]
                scores_new = jnp.where(later, NEGATIVE, scores_new)
                top = jnp.maximum(
                    jnp.max(scores_cache, axis=1, keepdims=True),
                    jnp.max(scores_new, axis=1, keepdims=True),
                )
                weights_cache = jnp.exp2((scores_cache - top) * exponent_scale)
                weights_new = jnp.exp2((scores_new - top) * exponent_scale)
                totals.append(
                    jnp.sum(weights_cache, axis=1, keepdims=True)
                    + jnp.sum(weights_new, axis=1, keepdims=True)
                )
                weights_all.append(weights_cache.astype(jnp.bfloat16))
                combined_new.append(
                    jnp.dot(
                        weights_new.astype(jnp.bfloat16),
                        projected[layer, rows, value_columns],
                        preferred_element_type=jnp.float32,
                    )
                )
            combined = jnp.dot(
                jnp.concatenate(weights_all, axis=0),
                cache_here[layer, 1, :, here],
                preferred_element_type=jnp.float32,
            )
            combined = (combined + jnp.concatenate(combined_new, axis=0)) / jnp.concatenate(
                totals, axis=0
            )
            attended[layer, column, span, here] = combined.astype(jnp.bfloat16)

    def share_heads(layer, first, count, rows, number):
        block = attended.at[layer, column, rows, first * HEAD : (first + count) * HEAD]
        copy = beside(block, block, 2 + layer * 4 + number)
        copy.start()
        sides.append(copy)
        return copy

    def mix(layer, carried, rows, after):
        for number in range(width // tile):
            columns = slice(number * tile, (number + 1) * tile)
            total = jnp.dot(
                attended[layer, 0, rows, :],
                out_rows[:width, columns],
                preferred_element_type=jnp.float32,
            )
            total += jnp.dot(
                attended[layer, 1, rows, :],
                out_rows[width:, columns],
                preferred_element_type=jnp.float32,
            )
            total = total + biases[0:1, columns] + carried[column, rows, columns].astype(jnp.float32)
            summed[layer, column, rows, columns] = total.astype(jnp.bfloat16)
            after(number, columns)

    def advance_early(kind):
        if kind == KEY:
            gather.step(OUT, 2)

    def advance(number):
        if number == 0:
            gather.step(OUT, 3)
        if number == 2:
            gather.step(OUT, 4)

    everything = slice(0, tokens)
    spans = [slice(request * SPAN, (request + 1) * SPAN) for request in range(requests)]
    project(0, inputs, everything, advance_early)
    stores = store_cache(0)
    group = heads // 4
    copies = []
    for number in range(4):
        attend_heads(0, number * group, group, 0, requests)
        copies.append(share_heads(0, number * group, group, everything, number))
        advance(number)
    gather.drain()
    gather.finish(OUT)
    for copy in copies:
        copy.wait_recv()

    exchanged = [[] for _ in spans]
    for request, rows in enumerate(spans):

        def share(number, columns, request=request, rows=rows):
            block = summed.at[0, column, rows, columns]
            copy = beside(block, block, 10 + 2 * request + number)
            copy.start()
            exchanged[request].append(copy)

        mix(0, inputs, rows, share)

    chunk = 64

    def norm_rows(j, carry):
        rows = pl.ds(pl.multiple_of(j * chunk, chunk), chunk)
        values = [summed[0, half, rows, :].astype(jnp.float32) for half in range(2)]
        means = sum(jnp.sum(v, axis=1, keepdims=True) for v in values) / full_width
        centered = [v - means for v in values]
        spread = sum(jnp.sum(c * c, axis=1, keepdims=True) for c in centered) / full_width
        inverse = lax.rsqrt(spread + EPSILON)
        for half in range(2):
            scaled = centered[half] * inverse
            scaled = scaled * scales_all[half, 0:1, :] + scales_all[half, 1:2, :]
            normed[half, rows, :] = scaled.astype(jnp.bfloat16)
        return carry


    half_heads = heads // 2
    copies = [[] for _ in spans]
    chunks = SPAN // chunk
    for request, rows in enumerate(spans):
        for copy in exchanged[request]:
            copy.wait_recv()
        sides += exchanged[request]
        lax.fori_loop(request * chunks, (request + 1) * chunks, norm_rows, 0)
        project(1, normed, rows, lambda kind: None)
        for number in range(2):
            attend_heads(1, number * half_heads, half_heads, request, request + 1)
            copies[request].append(
                share_heads(1, number * half_heads, half_heads, rows, 2 * request + number)
            )
    stores += store_cache(1)

    lane = lax.broadcasted_iota(jnp.int32, (chunk, 128), 1)

    def stat_rows(j, carry):
        rows = pl.ds(pl.multiple_of(j * chunk, chunk), chunk)
        values = summed[1, column, rows, :].astype(jnp.float32)
        mean = jnp.sum(values, axis=1, keepdims=True) / width
        centered = values - mean
        spread = jnp.sum(centered * centered, axis=1, keepdims=True)
        stats_wide[0, rows, :] = jnp.where(lane == 0, mean, jnp.where(lane == 1, spread, 0.0))
        return carry

    for request, rows in enumerate(spans):
        for copy in copies[request]:
            copy.wait_recv()
        mix(1, normed, rows, lambda number, columns: None)
        lax.fori_loop(request * chunks, (request + 1) * chunks, stat_rows, 0)
    stats[column] = jnp.transpose(stats_wide[0])[:8, :]
    send_stats = beside(stats.at[column], stats.at[column], 14)
    send_stats.start()
    send_stats.wait_recv()
    sides.append(send_stats)
    for half in range(2):
        padded = jnp.concatenate([stats[half], jnp.zeros((120, tokens), jnp.float32)], axis=0)
        stats_wide[half] = jnp.transpose(padded)

    def last_rows(j, carry):
        rows = pl.ds(pl.multiple_of(j * chunk, chunk), chunk)
        mean_a, mean_b = stats_wide[0, rows, 0:1], stats_wide[1, rows, 0:1]
        means = (mean_a + mean_b) * 0.5
        gap = mean_a - mean_b
        spread = stats_wide[0, rows, 1:2] + stats_wide[1, rows, 1:2] + gap * gap * (width * 0.5)
        inverse = lax.rsqrt(spread / full_width + EPSILON)
        scaled = (summed[1, column, rows, :].astype(jnp.float32) - means) * inverse
        scaled = scaled * scales_all[column, 0:1, :] + scales_all[column, 1:2, :]
        hidden_out[rows, :] = scaled.astype(jnp.bfloat16)
        return carry

    lax.fori_loop(0, tokens // chunk, last_rows, 0)

    for store in stores:
        store.wait()
    for copy in sides:
        copy.wait_send()


def fused(
    hidden_in,
    cache_lengths,
    cache_offsets,
    cache_kv,
    w_qkv,
    qkv_bias,
    w_out,
    out_bias,
    norm_gain,
    norm_shift,
):
    tokens, width = hidden_in.shape
    cache_count = cache_kv.shape[2]
    shard_rows = w_qkv.shape[0]
    depth = shard_rows * lax.axis_size("wide")
    requests = cache_lengths.shape[0]
    vmem = pl.BlockSpec(memory_space=pltpu.VMEM)
    hbm = pl.BlockSpec(memory_space=pltpu.HBM)
    operands = (
        cache_lengths,
        cache_offsets,
        hidden_in,
        cache_kv,
        jnp.transpose(w_qkv, (1, 0, 2)),
        w_out,
        qkv_bias,
        out_bias,
        norm_gain,
        norm_shift,
    )
    anywhere = pl.BlockSpec(memory_space=pl.ANY)
    bf16 = jnp.bfloat16
    return pl.pallas_call(
        fused_kernel,
        out_shape=(
            jax.ShapeDtypeStruct((tokens, width), bf16),
            jax.ShapeDtypeStruct((LAYERS, 2, tokens, width), bf16),
        ),
        in_specs=[hbm] * 10,
        out_specs=(vmem, anywhere),
        scratch_shapes=[
            pltpu.SMEM((requests,), jnp.int32),
            pltpu.SMEM((requests,), jnp.int32),
            pltpu.VMEM((3, width), bf16),
            pltpu.VMEM((width,), bf16),
            pltpu.VMEM((width,), bf16),
            pltpu.VMEM((width,), bf16),
            pltpu.VMEM((depth, 3 * width), bf16),
            pltpu.VMEM((depth, width), bf16),
            pltpu.VMEM((LAYERS, 2, cache_count, width), bf16),
            pltpu.VMEM((2, tokens, width), bf16),
            pltpu.VMEM((LAYERS, tokens, 3 * width), bf16),
            pltpu.VMEM((LAYERS, 2, tokens, width), bf16),
            pltpu.VMEM((LAYERS, 2, tokens, width), bf16),
            pltpu.VMEM((2, tokens, width), bf16),
            pltpu.VMEM((2, 8, width), jnp.float32),
            pltpu.VMEM((8, width), jnp.float32),
            pltpu.VMEM((2, 8, tokens), jnp.float32),
            pltpu.VMEM((2, tokens, 128), jnp.float32),
            pltpu.VMEM((requests, 8, cache_count), jnp.float32),
            pltpu.SemaphoreType.DMA((4, 2, CHIPS_Z * CHIPS_Y, 4)),
            pltpu.SemaphoreType.DMA((4, 2, CHIPS_Z * CHIPS_Y * CORES)),
            pltpu.SemaphoreType.DMA((18,)),
            pltpu.SemaphoreType.DMA((15,)),
            pltpu.SemaphoreType.DMA((15,)),
        ],
        compiler_params=pltpu.CompilerParams(
            collective_id=0, has_side_effects=True, vmem_limit_bytes=VMEM_BYTES
        ),
        cost_estimate=pl.CostEstimate(
            flops=2 * LAYERS * tokens * depth * 4 * width,
            bytes_accessed=2 * depth * 4 * width,
            transcendentals=LAYERS * tokens * cache_count * (width // HEAD),
        ),
    )(*(pltpu.with_memory_space_constraint(operand, pltpu.HBM) for operand in operands))


def solution(mesh):
    in_specs = (
        P("wide", "narrow"),
        P("wide"),
        P("wide"),
        P(None, None, "wide", "narrow"),
        P("wide", None, "narrow"),
        P(None, "narrow"),
        P("wide", "narrow"),
        P("narrow"),
        P("narrow"),
        P("narrow"),
    )
    out_specs = (P("wide", "narrow"), P(None, None, "wide", "narrow"))
    body = fused if fits_fused(mesh) else shards
    return jax.shard_map(body, mesh=mesh, in_specs=in_specs, out_specs=out_specs, check_vma=False)
```

```python
import functools
import math

import jax
import jax.numpy as jnp
from jax import lax
from jax.experimental import pallas as pl
from jax.experimental.pallas import tpu as pltpu
from jax.sharding import PartitionSpec as P

HEAD = 128
SPAN = 128
LAYERS = 2


EPSILON = 1e-05
NEGATIVE = -1e30


def add_rows(shard_piece, operand):
    piece_rows = shard_piece.shape[0]
    return jnp.dot(operand, shard_piece.reshape(piece_rows, -1), preferred_element_type=jnp.float32)


def norm_slice(summed, norm_gain, norm_shift, full_width):
    values = summed.astype(jnp.float32)
    row_means = lax.psum(jnp.sum(values, axis=1), "narrow") / full_width
    centered = values - row_means[:, None]
    row_spread = lax.psum(jnp.sum(centered * centered, axis=1), "narrow") / full_width
    scaled = centered * lax.rsqrt(row_spread[:, None] + EPSILON)
    return (scaled * norm_gain.astype(jnp.float32) + norm_shift.astype(jnp.float32)).astype(
        jnp.bfloat16
    )


def attend(queries, keys_new, values_new, keys_cache, values_cache, live_cache, live_new):
    scale_factor = 1.0 / math.sqrt(queries.shape[2])
    scores_cache = (
        jnp.einsum("qhd,khd->hqk", queries, keys_cache, preferred_element_type=jnp.float32)
        * scale_factor
    )
    scores_new = (
        jnp.einsum("qhd,khd->hqk", queries, keys_new, preferred_element_type=jnp.float32)
        * scale_factor
    )
    masked_cache = jnp.where(live_cache[None], scores_cache, NEGATIVE)
    masked_new = jnp.where(live_new[None], scores_new, NEGATIVE)
    top_score = jnp.maximum(jnp.max(masked_cache, axis=2), jnp.max(masked_new, axis=2))[:, :, None]
    weights_cache = jnp.where(live_cache[None], jnp.exp(masked_cache - top_score), 0.0)
    weights_new = jnp.where(live_new[None], jnp.exp(masked_new - top_score), 0.0)
    totals = jnp.sum(weights_cache, axis=2, keepdims=True) + jnp.sum(
        weights_new, axis=2, keepdims=True
    )
    probs_cache = (weights_cache / totals).astype(jnp.bfloat16)
    probs_new = (weights_new / totals).astype(jnp.bfloat16)
    combined = jnp.einsum(
        "hqk,khd->qhd", probs_cache, values_cache, preferred_element_type=jnp.float32
    )
    combined = combined + jnp.einsum(
        "hqk,khd->qhd", probs_new, values_new, preferred_element_type=jnp.float32
    )
    return combined.astype(jnp.bfloat16).reshape(queries.shape[0], -1)


def shards(
    hidden_in,
    cache_lengths,
    cache_offsets,
    cache_kv,
    w_qkv,
    qkv_bias,
    w_out,
    out_bias,
    norm_gain,
    norm_shift,
):
    row_count, local_width = hidden_in.shape
    full_width = local_width * lax.axis_size("narrow")
    local_heads = local_width // HEAD
    cache_count = cache_kv.shape[2]
    requests_here = cache_lengths.shape[0]
    block_start = lax.axis_index("wide") * cache_count
    rows_global = block_start + jnp.arange(cache_count, dtype=jnp.int32)
    row_start = jnp.broadcast_to(cache_offsets[:, None], (requests_here, SPAN)).reshape(-1)
    row_stop = row_start + jnp.broadcast_to(cache_lengths[:, None], (requests_here, SPAN)).reshape(
        -1
    )
    live_cache = (rows_global[None, :] >= row_start[:, None]) & (
        rows_global[None, :] < row_stop[:, None]
    )
    owner_index = jnp.arange(row_count, dtype=jnp.int32) // SPAN
    position = jnp.arange(row_count, dtype=jnp.int32) % SPAN
    live_new = (owner_index[:, None] == owner_index[None, :]) & (
        position[:, None] >= position[None, :]
    )
    bias_flat = qkv_bias.astype(jnp.float32).reshape(-1)
    gathered = lax.all_gather(hidden_in, "narrow", axis=1, tiled=True)
    carried = hidden_in
    appended = []
    for layer_index in range(LAYERS):
        projections = add_rows(lax.all_gather(w_qkv, "wide", axis=0, tiled=True), operand=gathered)
        projections = projections + bias_flat
        queries = projections[:, :local_width].astype(jnp.bfloat16)
        keys_new = projections[:, local_width : 2 * local_width].astype(jnp.bfloat16)
        values_new = projections[:, 2 * local_width :].astype(jnp.bfloat16)
        appended.append(jnp.stack([keys_new, values_new]))
        keys_cache = cache_kv[layer_index, 0].reshape(cache_count, local_heads, HEAD)
        values_cache = cache_kv[layer_index, 1].reshape(cache_count, local_heads, HEAD)
        attended = attend(
            queries.reshape(row_count, local_heads, HEAD),
            keys_new.reshape(row_count, local_heads, HEAD),
            values_new.reshape(row_count, local_heads, HEAD),
            keys_cache,
            values_cache,
            live_cache,
            live_new,
        )
        heads_all = lax.all_gather(attended, "narrow", axis=1, tiled=True)
        projected = add_rows(lax.all_gather(w_out, "wide", axis=0, tiled=True), operand=heads_all)
        summed = (projected + out_bias.astype(jnp.float32) + carried.astype(jnp.float32)).astype(
            jnp.bfloat16
        )
        if layer_index + 1 < LAYERS:
            carried = norm_slice(summed, norm_gain, norm_shift, full_width)
            gathered = lax.all_gather(carried, "narrow", axis=1, tiled=True)
        else:
            carried = norm_slice(summed, norm_gain, norm_shift, full_width)
    return (carried, jnp.stack(appended))


MESH = pl.DeviceIdType.MESH
CHIPS_Y = 2
CHIPS_Z = 4
CORES = 2
UP, DOWN, ACROSS, SIBLING = range(4)
QUERY, KEY, VALUE, OUT = range(4)
QKV = (QUERY, KEY, VALUE)
FIRST, SECOND = range(2)
VMEM_BYTES = 48 * 1024 * 1024


def fits_fused(mesh):
    return mesh.shape["wide"] == CHIPS_Z * CHIPS_Y * CORES and mesh.shape["narrow"] == 2


class Gather:
    def __init__(self, buffers, shard_rows, cuts, send_sem, recv_sem):
        self.buffers, self.shard_rows, self.cuts = buffers, shard_rows, cuts
        self.send_sem, self.recv_sem = send_sem, recv_sem
        me = lax.axis_index("wide")
        self.core = lax.rem(me, CORES)
        self.y = lax.rem(me // CORES, CHIPS_Y)
        self.z = me // (CORES * CHIPS_Y)
        self.me = me
        self.targets = {
            UP: (self.z + 1 < CHIPS_Z, me + CORES * CHIPS_Y),
            DOWN: (self.z > 0, me - CORES * CHIPS_Y),
            ACROSS: (True, self.index(self.z, 1 - self.y, self.core)),
            SIBLING: (True, self.index(self.z, self.y, 1 - self.core)),
        }
        self.pending = []

    def index(self, z, y, core):
        return (z * CHIPS_Y + y) * CORES + core

    def slot(self, which, part, source):
        cut = self.cuts[which]
        start = source * self.shard_rows + (0 if part == FIRST else cut)
        size = cut if part == FIRST else self.shard_rows - cut
        buffer, columns = self.buffers[which]
        return buffer.at[pl.ds(pl.multiple_of(start, 16), size), columns]

    def copy(self, which, part, z, y, core, kind):
        source = self.index(z, y, core)
        block = self.slot(which, part, source)
        return pltpu.make_async_remote_copy(
            src_ref=block,
            dst_ref=block,
            send_sem=self.send_sem.at[which, part, z * CHIPS_Y + y, kind],
            recv_sem=self.recv_sem.at[which, part, source],
            device_id={"wide": self.targets[kind][1]},
            device_id_type=MESH,
        )

    def send(self, which, part, z, y, kinds, valid=True):
        for kind in kinds:
            condition = self.targets[kind][0]
            if condition is True:
                condition = valid
            elif valid is not True:
                condition = jnp.logical_and(condition, valid)
            make = functools.partial(self.copy, which, part, z, y, self.core, kind)
            self.when(condition, lambda make=make: make().start())
            self.pending.append((condition, make))

    def when(self, condition, action):
        if condition is True:
            action()
        else:
            pl.when(condition)(action)

    def arrive(self, which, part, z, y, core, valid=True):
        make = functools.partial(self.copy, which, part, z, y, core, SIBLING)
        self.when(valid, lambda: make().wait_recv())

    def begin(self, which):
        z, y = self.z, self.y
        self.send(which, SECOND, z, y, (ACROSS,))
        self.send(which, FIRST, z, y, (UP, DOWN, ACROSS))
        self.send(which, SECOND, z, y, (UP, DOWN))
        self.send(which, FIRST, z, y, (SIBLING,))
        self.send(which, SECOND, z, y, (SIBLING,))

    def around(self, distance):
        low, high = self.z - distance, self.z + distance
        return ((low, low >= 0, UP), (high, high < CHIPS_Z, DOWN))

    def take_across(self, which, distance):
        y = 1 - self.y
        places = ((self.z, True, None),) if distance == 0 else self.around(distance)
        for z, valid, _ in places:
            self.arrive(which, FIRST, z, y, self.core, valid)
            self.send(which, FIRST, z, y, (SIBLING,), valid)

    def step(self, which, distance):
        if distance == 0:
            y = 1 - self.y
            self.arrive(which, SECOND, self.z, y, self.core)
            self.send(which, SECOND, self.z, y, (UP, DOWN, SIBLING))
            return
        if distance < CHIPS_Z:
            for z, valid, onward in self.around(distance):
                self.arrive(which, FIRST, z, self.y, self.core, valid)
                self.send(which, FIRST, z, self.y, (onward, ACROSS, SIBLING), valid)
            for z, valid, onward in self.around(distance):
                for y in (self.y, 1 - self.y):
                    self.arrive(which, SECOND, z, y, self.core, valid)
                    self.send(which, SECOND, z, y, (onward, SIBLING), valid)
        self.take_across(which, distance - 1)

    def finish(self, which):
        for part in (FIRST, SECOND):
            for z in range(CHIPS_Z):
                for y in range(CHIPS_Y):
                    self.arrive(which, part, z, y, 1 - self.core)

    def drain(self):
        for condition, make in self.pending:
            self.when(condition, lambda make=make: make().wait_send())
        self.pending = []


def fused_kernel(
    lengths_in,
    offsets_in,
    hidden,
    cache,
    w_qkv,
    w_out,
    qkv_bias_in,
    out_bias_in,
    norm_gain_in,
    norm_shift_in,
    hidden_out,
    new_cache,
    lengths,
    offsets,
    qkv_bias,
    out_bias,
    norm_gain,
    norm_shift,
    qkv_rows,
    out_rows,
    cache_here,
    inputs,
    projected,
    attended,
    summed,
    normed,
    scales_all,
    biases,
    stats,
    stats_wide,
    live,
    send_sem,
    recv_sem,
    local_sem,
    side_send,
    side_recv,
):
    tokens, width = hidden.shape
    cache_count = cache.shape[2]
    requests = lengths.shape[0]
    shard_rows = w_out.shape[0]
    heads = width // HEAD
    full_width = 2 * width
    column = lax.axis_index("narrow")
    other = 1 - column
    buffers = [(qkv_rows, slice(kind * width, (kind + 1) * width)) for kind in QKV]
    buffers.append((out_rows, slice(0, width)))
    gather = Gather(buffers, shard_rows, (112, 112, 112, 96), send_sem, recv_sem)

    barrier = pltpu.get_barrier_semaphore()
    for condition, target in gather.targets.values():

        def greet(target=target):
            pl.semaphore_signal(
                barrier, inc=1, device_id={"wide": target}, device_id_type=MESH
            )

        gather.when(condition, greet)
    pl.semaphore_signal(barrier, inc=1, device_id={"narrow": other}, device_id_type=MESH)

    own_rows = pl.ds(pl.multiple_of(gather.me * shard_rows, 16), shard_rows)
    load_qkv = [
        pltpu.make_async_copy(
            w_qkv.at[kind], qkv_rows.at[own_rows, buffers[kind][1]], local_sem.at[9 + kind]
        )
        for kind in QKV
    ]
    load_out = pltpu.make_async_copy(w_out, out_rows.at[own_rows, :], local_sem.at[1])
    load_hidden = pltpu.make_async_copy(hidden, inputs.at[column], local_sem.at[2])
    load_cache = pltpu.make_async_copy(cache, cache_here, local_sem.at[3])
    pairs = (
        (lengths_in, lengths),
        (offsets_in, offsets),
        (qkv_bias_in, qkv_bias),
        (out_bias_in, out_bias),
        (norm_gain_in, norm_gain),
        (norm_shift_in, norm_shift),
    )
    load_small = [
        pltpu.make_async_copy(source, target, local_sem.at[12 + number])
        for number, (source, target) in enumerate(pairs)
    ]
    for load in (*load_qkv, load_hidden, load_out, *load_small, load_cache):
        load.start()

    has_lower = (gather.z + CHIPS_Z - 1) // CHIPS_Z
    has_upper = (2 * CHIPS_Z - 2 - gather.z) // CHIPS_Z
    pl.semaphore_wait(barrier, 3 + has_lower + has_upper)

    def beside(source, target, number):
        return pltpu.make_async_remote_copy(
            src_ref=source,
            dst_ref=target,
            send_sem=side_send.at[number],
            recv_sem=side_recv.at[number],
            device_id={"narrow": other},
            device_id_type=MESH,
        )

    for kind in QKV:
        load_qkv[kind].wait()
        gather.begin(kind)
    load_hidden.wait()
    for load in load_small:
        load.wait()
    scales_all[column, 0:1, :] = norm_gain[...].astype(jnp.float32).reshape(1, width)
    scales_all[column, 1:2, :] = norm_shift[...].astype(jnp.float32).reshape(1, width)
    scales_all[column, 2:8, :] = jnp.zeros((6, width), jnp.float32)
    biases[0:1, :] = out_bias[...].astype(jnp.float32).reshape(1, width)
    for kind in QKV:
        biases[kind + 1 : kind + 2, :] = qkv_bias[kind : kind + 1, :].astype(jnp.float32)
    send_hidden = beside(inputs.at[column], inputs.at[column], 0)
    send_scales = beside(scales_all.at[column], scales_all.at[column], 1)
    send_hidden.start()
    send_scales.start()
    load_out.wait()
    sides = [send_hidden, send_scales]

    block_start = gather.me * cache_count
    rows_global = block_start + lax.broadcasted_iota(jnp.int32, (8, cache_count), 1)
    for request in range(requests):
        start = offsets[request]
        stop = start + lengths[request]
        alive = jnp.logical_and(rows_global >= start, rows_global < stop)
        live[request] = jnp.where(alive, 0.0, NEGATIVE)
    later = lax.broadcasted_iota(jnp.int32, (SPAN, SPAN), 0) < lax.broadcasted_iota(
        jnp.int32, (SPAN, SPAN), 1
    )
    scale_factor = 1.0 / math.sqrt(HEAD)

    for distance in range(CHIPS_Z):
        for kind in QKV:
            gather.step(kind, distance)
    gather.begin(OUT)
    send_hidden.wait_recv()
    send_scales.wait_recv()
    load_cache.wait()

    tile = 512

    def project(layer, source, rows, before):
        for kind in QKV:
            before(kind)

            def one(j, carry, kind=kind):
                here = pl.ds(pl.multiple_of(j * tile, tile), tile)
                columns = pl.ds(pl.multiple_of(kind * width + j * tile, tile), tile)
                total = jnp.dot(
                    source[0, rows, :], qkv_rows[:width, columns], preferred_element_type=jnp.float32
                )
                total += jnp.dot(
                    source[1, rows, :], qkv_rows[width:, columns], preferred_element_type=jnp.float32
                )
                total = total + biases[kind + 1 : kind + 2, here]
                projected[layer, rows, columns] = total.astype(jnp.bfloat16)
                return carry

            lax.fori_loop(0, width // tile, one, 0)

    def store_cache(layer):
        stores = []
        for kind in range(2):
            block = projected.at[layer, :, (kind + 1) * width : (kind + 2) * width]
            store = pltpu.make_async_copy(
                block, new_cache.at[layer, kind], local_sem.at[5 + 2 * layer + kind]
            )
            store.start()
            stores.append(store)
        return stores

    contract = (((1,), (1,)), ((), ()))
    exponent_scale = scale_factor * math.log2(math.e)

    def with_ones(values):
        return jnp.concatenate([values, jnp.ones_like(values)], axis=1)

    def attend_heads(layer, first, count, first_request, last_request):
        span = slice(first_request * SPAN, last_request * SPAN)
        for head in range(first, first + count):
            here = slice(head * HEAD, (head + 1) * HEAD)
            key_columns = slice(width + head * HEAD, width + (head + 1) * HEAD)
            value_columns = slice(2 * width + head * HEAD, 2 * width + (head + 1) * HEAD)
            scores_all = lax.dot_general(
                projected[layer, span, here],
                cache_here[layer, 0, :, here],
                contract,
                preferred_element_type=jnp.float32,
            )
            weights_all, combined_new = [], []
            for request in range(first_request, last_request):
                rows = slice(request * SPAN, (request + 1) * SPAN)
                within = request - first_request
                scores_new = lax.dot_general(
                    projected[layer, rows, here],
                    projected[layer, rows, key_columns],
                    contract,
                    preferred_element_type=jnp.float32,
                )
                scores_cache = scores_all[within * SPAN : (within + 1) * SPAN, :] + live[request, 0:1, :]
                scores_new = jnp.where(later, NEGATIVE, scores_new)
                top = jnp.maximum(
                    jnp.max(scores_cache, axis=1, keepdims=True),
                    jnp.max(scores_new, axis=1, keepdims=True),
                )
                weights_cache = jnp.exp2((scores_cache - top) * exponent_scale)
                weights_new = jnp.exp2((scores_new - top) * exponent_scale)
                weights_all.append(weights_cache.astype(jnp.bfloat16))
                combined_new.append(
                    jnp.dot(
                        weights_new.astype(jnp.bfloat16),
                        with_ones(projected[layer, rows, value_columns]),
                        preferred_element_type=jnp.float32,
                    )
                )
            combined = jnp.dot(
                jnp.concatenate(weights_all, axis=0),
                with_ones(cache_here[layer, 1, :, here]),
                preferred_element_type=jnp.float32,
            )
            combined = combined + jnp.concatenate(combined_new, axis=0)
            combined = combined[:, :HEAD] / combined[:, HEAD:]
            attended[layer, column, span, here] = combined.astype(jnp.bfloat16)

    def share_heads(layer, first, count, rows, number):
        block = attended.at[layer, column, rows, first * HEAD : (first + count) * HEAD]
        copy = beside(block, block, 2 + layer * 4 + number)
        copy.start()
        sides.append(copy)
        return copy

    def mix(layer, carried, rows, after):
        for number in range(width // tile):
            columns = slice(number * tile, (number + 1) * tile)
            total = jnp.dot(
                attended[layer, 0, rows, :],
                out_rows[:width, columns],
                preferred_element_type=jnp.float32,
            )
            total += jnp.dot(
                attended[layer, 1, rows, :],
                out_rows[width:, columns],
                preferred_element_type=jnp.float32,
            )
            total = total + biases[0:1, columns] + carried[column, rows, columns].astype(jnp.float32)
            summed[layer, column, rows, columns] = total.astype(jnp.bfloat16)
            after(number, columns)

    def advance_early(kind):
        gather.step(kind, CHIPS_Z)
        gather.finish(kind)
        if kind == VALUE:
            gather.step(OUT, 0)
            gather.step(OUT, 1)

    def advance(number):
        gather.step(OUT, number + 2)

    everything = slice(0, tokens)
    spans = [slice(request * SPAN, (request + 1) * SPAN) for request in range(requests)]
    project(0, inputs, everything, advance_early)
    stores = store_cache(0)
    group = heads // 4
    copies = []
    for number in range(4):
        if number < 3:
            advance(number)
        attend_heads(0, number * group, group, 0, requests)
        copies.append(share_heads(0, number * group, group, everything, number))
    gather.finish(OUT)
    for copy in copies:
        copy.wait_recv()

    exchanged = [[] for _ in spans]
    for request, rows in enumerate(spans):

        def share(number, columns, request=request, rows=rows):
            block = summed.at[0, column, rows, columns]
            copy = beside(block, block, 10 + 2 * request + number)
            copy.start()
            exchanged[request].append(copy)

        mix(0, inputs, rows, share)
    gather.drain()

    chunk = 64

    def norm_rows(j, carry):
        rows = pl.ds(pl.multiple_of(j * chunk, chunk), chunk)
        values = [summed[0, half, rows, :].astype(jnp.float32) for half in range(2)]
        means = sum(jnp.sum(v, axis=1, keepdims=True) for v in values) / full_width
        centered = [v - means for v in values]
        spread = sum(jnp.sum(c * c, axis=1, keepdims=True) for c in centered) / full_width
        inverse = lax.rsqrt(spread + EPSILON)
        for half in range(2):
            scaled = centered[half] * inverse
            scaled = scaled * scales_all[half, 0:1, :] + scales_all[half, 1:2, :]
            normed[half, rows, :] = scaled.astype(jnp.bfloat16)
        return carry


    half_heads = heads // 2
    copies = [[] for _ in spans]
    chunks = SPAN // chunk
    for request, rows in enumerate(spans):
        for copy in exchanged[request]:
            copy.wait_recv()
        sides += exchanged[request]
        lax.fori_loop(request * chunks, (request + 1) * chunks, norm_rows, 0)
        project(1, normed, rows, lambda kind: None)
        for number in range(2):
            attend_heads(1, number * half_heads, half_heads, request, request + 1)
            copies[request].append(
                share_heads(1, number * half_heads, half_heads, rows, 2 * request + number)
            )
    stores += store_cache(1)

    lane = lax.broadcasted_iota(jnp.int32, (chunk, 128), 1)

    def stat_rows(j, carry):
        rows = pl.ds(pl.multiple_of(j * chunk, chunk), chunk)
        values = summed[1, column, rows, :].astype(jnp.float32)
        mean = jnp.sum(values, axis=1, keepdims=True) / width
        centered = values - mean
        spread = jnp.sum(centered * centered, axis=1, keepdims=True)
        stats_wide[0, rows, :] = jnp.where(lane == 0, mean, jnp.where(lane == 1, spread, 0.0))
        return carry

    for request, rows in enumerate(spans):
        for copy in copies[request]:
            copy.wait_recv()
        mix(1, normed, rows, lambda number, columns: None)
        lax.fori_loop(request * chunks, (request + 1) * chunks, stat_rows, 0)
    stats[column] = jnp.transpose(stats_wide[0])[:8, :]
    send_stats = beside(stats.at[column], stats.at[column], 14)
    send_stats.start()
    send_stats.wait_recv()
    sides.append(send_stats)
    for half in range(2):
        padded = jnp.concatenate([stats[half], jnp.zeros((120, tokens), jnp.float32)], axis=0)
        stats_wide[half] = jnp.transpose(padded)

    def last_rows(j, carry):
        rows = pl.ds(pl.multiple_of(j * chunk, chunk), chunk)
        mean_a, mean_b = stats_wide[0, rows, 0:1], stats_wide[1, rows, 0:1]
        means = (mean_a + mean_b) * 0.5
        gap = mean_a - mean_b
        spread = stats_wide[0, rows, 1:2] + stats_wide[1, rows, 1:2] + gap * gap * (width * 0.5)
        inverse = lax.rsqrt(spread / full_width + EPSILON)
        scaled = (summed[1, column, rows, :].astype(jnp.float32) - means) * inverse
        scaled = scaled * scales_all[column, 0:1, :] + scales_all[column, 1:2, :]
        hidden_out[rows, :] = scaled.astype(jnp.bfloat16)
        return carry

    lax.fori_loop(0, tokens // chunk, last_rows, 0)

    for store in stores:
        store.wait()
    for copy in sides:
        copy.wait_send()


def fused(
    hidden_in,
    cache_lengths,
    cache_offsets,
    cache_kv,
    w_qkv,
    qkv_bias,
    w_out,
    out_bias,
    norm_gain,
    norm_shift,
):
    tokens, width = hidden_in.shape
    cache_count = cache_kv.shape[2]
    shard_rows = w_qkv.shape[0]
    depth = shard_rows * lax.axis_size("wide")
    requests = cache_lengths.shape[0]
    vmem = pl.BlockSpec(memory_space=pltpu.VMEM)
    hbm = pl.BlockSpec(memory_space=pltpu.HBM)
    operands = (
        cache_lengths,
        cache_offsets,
        hidden_in,
        cache_kv,
        jnp.transpose(w_qkv, (1, 0, 2)),
        w_out,
        qkv_bias,
        out_bias,
        norm_gain,
        norm_shift,
    )
    anywhere = pl.BlockSpec(memory_space=pl.ANY)
    bf16 = jnp.bfloat16
    return pl.pallas_call(
        fused_kernel,
        out_shape=(
            jax.ShapeDtypeStruct((tokens, width), bf16),
            jax.ShapeDtypeStruct((LAYERS, 2, tokens, width), bf16),
        ),
        in_specs=[hbm] * 10,
        out_specs=(vmem, anywhere),
        scratch_shapes=[
            pltpu.SMEM((requests,), jnp.int32),
            pltpu.SMEM((requests,), jnp.int32),
            pltpu.VMEM((3, width), bf16),
            pltpu.VMEM((width,), bf16),
            pltpu.VMEM((width,), bf16),
            pltpu.VMEM((width,), bf16),
            pltpu.VMEM((depth, 3 * width), bf16),
            pltpu.VMEM((depth, width), bf16),
            pltpu.VMEM((LAYERS, 2, cache_count, width), bf16),
            pltpu.VMEM((2, tokens, width), bf16),
            pltpu.VMEM((LAYERS, tokens, 3 * width), bf16),
            pltpu.VMEM((LAYERS, 2, tokens, width), bf16),
            pltpu.VMEM((LAYERS, 2, tokens, width), bf16),
            pltpu.VMEM((2, tokens, width), bf16),
            pltpu.VMEM((2, 8, width), jnp.float32),
            pltpu.VMEM((8, width), jnp.float32),
            pltpu.VMEM((2, 8, tokens), jnp.float32),
            pltpu.VMEM((2, tokens, 128), jnp.float32),
            pltpu.VMEM((requests, 8, cache_count), jnp.float32),
            pltpu.SemaphoreType.DMA((4, 2, CHIPS_Z * CHIPS_Y, 4)),
            pltpu.SemaphoreType.DMA((4, 2, CHIPS_Z * CHIPS_Y * CORES)),
            pltpu.SemaphoreType.DMA((18,)),
            pltpu.SemaphoreType.DMA((15,)),
            pltpu.SemaphoreType.DMA((15,)),
        ],
        compiler_params=pltpu.CompilerParams(
            collective_id=0, has_side_effects=True, vmem_limit_bytes=VMEM_BYTES
        ),
        cost_estimate=pl.CostEstimate(
            flops=2 * LAYERS * tokens * depth * 4 * width,
            bytes_accessed=2 * depth * 4 * width,
            transcendentals=LAYERS * tokens * cache_count * (width // HEAD),
        ),
    )(*(pltpu.with_memory_space_constraint(operand, pltpu.HBM) for operand in operands))


def solution(mesh):
    in_specs = (
        P("wide", "narrow"),
        P("wide"),
        P("wide"),
        P(None, None, "wide", "narrow"),
        P("wide", None, "narrow"),
        P(None, "narrow"),
        P("wide", "narrow"),
        P("narrow"),
        P("narrow"),
        P("narrow"),
    )
    out_specs = (P("wide", "narrow"), P(None, None, "wide", "narrow"))
    body = fused if fits_fused(mesh) else shards
    return jax.shard_map(body, mesh=mesh, in_specs=in_specs, out_specs=out_specs, check_vma=False)
```

```python
import functools
import math

import jax
import jax.numpy as jnp
from jax import lax
from jax.experimental import pallas as pl
from jax.experimental.pallas import tpu as pltpu
from jax.sharding import PartitionSpec as P

HEAD = 128
SPAN = 128
LAYERS = 2


EPSILON = 1e-05
NEGATIVE = -1e30


def add_rows(shard_piece, operand):
    piece_rows = shard_piece.shape[0]
    return jnp.dot(operand, shard_piece.reshape(piece_rows, -1), preferred_element_type=jnp.float32)


def norm_slice(summed, norm_gain, norm_shift, full_width):
    values = summed.astype(jnp.float32)
    row_means = lax.psum(jnp.sum(values, axis=1), "narrow") / full_width
    centered = values - row_means[:, None]
    row_spread = lax.psum(jnp.sum(centered * centered, axis=1), "narrow") / full_width
    scaled = centered * lax.rsqrt(row_spread[:, None] + EPSILON)
    return (scaled * norm_gain.astype(jnp.float32) + norm_shift.astype(jnp.float32)).astype(
        jnp.bfloat16
    )


def attend(queries, keys_new, values_new, keys_cache, values_cache, live_cache, live_new):
    scale_factor = 1.0 / math.sqrt(queries.shape[2])
    scores_cache = (
        jnp.einsum("qhd,khd->hqk", queries, keys_cache, preferred_element_type=jnp.float32)
        * scale_factor
    )
    scores_new = (
        jnp.einsum("qhd,khd->hqk", queries, keys_new, preferred_element_type=jnp.float32)
        * scale_factor
    )
    masked_cache = jnp.where(live_cache[None], scores_cache, NEGATIVE)
    masked_new = jnp.where(live_new[None], scores_new, NEGATIVE)
    top_score = jnp.maximum(jnp.max(masked_cache, axis=2), jnp.max(masked_new, axis=2))[:, :, None]
    weights_cache = jnp.where(live_cache[None], jnp.exp(masked_cache - top_score), 0.0)
    weights_new = jnp.where(live_new[None], jnp.exp(masked_new - top_score), 0.0)
    totals = jnp.sum(weights_cache, axis=2, keepdims=True) + jnp.sum(
        weights_new, axis=2, keepdims=True
    )
    probs_cache = (weights_cache / totals).astype(jnp.bfloat16)
    probs_new = (weights_new / totals).astype(jnp.bfloat16)
    combined = jnp.einsum(
        "hqk,khd->qhd", probs_cache, values_cache, preferred_element_type=jnp.float32
    )
    combined = combined + jnp.einsum(
        "hqk,khd->qhd", probs_new, values_new, preferred_element_type=jnp.float32
    )
    return combined.astype(jnp.bfloat16).reshape(queries.shape[0], -1)


def shards(
    hidden_in,
    cache_lengths,
    cache_offsets,
    cache_kv,
    w_qkv,
    qkv_bias,
    w_out,
    out_bias,
    norm_gain,
    norm_shift,
):
    row_count, local_width = hidden_in.shape
    full_width = local_width * lax.axis_size("narrow")
    local_heads = local_width // HEAD
    cache_count = cache_kv.shape[2]
    requests_here = cache_lengths.shape[0]
    block_start = lax.axis_index("wide") * cache_count
    rows_global = block_start + jnp.arange(cache_count, dtype=jnp.int32)
    row_start = jnp.broadcast_to(cache_offsets[:, None], (requests_here, SPAN)).reshape(-1)
    row_stop = row_start + jnp.broadcast_to(cache_lengths[:, None], (requests_here, SPAN)).reshape(
        -1
    )
    live_cache = (rows_global[None, :] >= row_start[:, None]) & (
        rows_global[None, :] < row_stop[:, None]
    )
    owner_index = jnp.arange(row_count, dtype=jnp.int32) // SPAN
    position = jnp.arange(row_count, dtype=jnp.int32) % SPAN
    live_new = (owner_index[:, None] == owner_index[None, :]) & (
        position[:, None] >= position[None, :]
    )
    bias_flat = qkv_bias.astype(jnp.float32).reshape(-1)
    gathered = lax.all_gather(hidden_in, "narrow", axis=1, tiled=True)
    carried = hidden_in
    appended = []
    for layer_index in range(LAYERS):
        projections = add_rows(lax.all_gather(w_qkv, "wide", axis=0, tiled=True), operand=gathered)
        projections = projections + bias_flat
        queries = projections[:, :local_width].astype(jnp.bfloat16)
        keys_new = projections[:, local_width : 2 * local_width].astype(jnp.bfloat16)
        values_new = projections[:, 2 * local_width :].astype(jnp.bfloat16)
        appended.append(jnp.stack([keys_new, values_new]))
        keys_cache = cache_kv[layer_index, 0].reshape(cache_count, local_heads, HEAD)
        values_cache = cache_kv[layer_index, 1].reshape(cache_count, local_heads, HEAD)
        attended = attend(
            queries.reshape(row_count, local_heads, HEAD),
            keys_new.reshape(row_count, local_heads, HEAD),
            values_new.reshape(row_count, local_heads, HEAD),
            keys_cache,
            values_cache,
            live_cache,
            live_new,
        )
        heads_all = lax.all_gather(attended, "narrow", axis=1, tiled=True)
        projected = add_rows(lax.all_gather(w_out, "wide", axis=0, tiled=True), operand=heads_all)
        summed = (projected + out_bias.astype(jnp.float32) + carried.astype(jnp.float32)).astype(
            jnp.bfloat16
        )
        if layer_index + 1 < LAYERS:
            carried = norm_slice(summed, norm_gain, norm_shift, full_width)
            gathered = lax.all_gather(carried, "narrow", axis=1, tiled=True)
        else:
            carried = norm_slice(summed, norm_gain, norm_shift, full_width)
    return (carried, jnp.stack(appended))


MESH = pl.DeviceIdType.MESH
CHIPS_Y = 2
CHIPS_Z = 4
CORES = 2
UP, DOWN, ACROSS, SIBLING = range(4)
QUERY, KEY, VALUE, OUT = range(4)
QKV = (QUERY, KEY, VALUE)
FIRST, SECOND = range(2)
VMEM_BYTES = 48 * 1024 * 1024


def fits_fused(mesh):
    return mesh.shape["wide"] == CHIPS_Z * CHIPS_Y * CORES and mesh.shape["narrow"] == 2


class Gather:
    def __init__(self, buffers, shard_rows, cuts, send_sem, recv_sem):
        self.buffers, self.shard_rows, self.cuts = buffers, shard_rows, cuts
        self.send_sem, self.recv_sem = send_sem, recv_sem
        me = lax.axis_index("wide")
        self.core = lax.rem(me, CORES)
        self.y = lax.rem(me // CORES, CHIPS_Y)
        self.z = me // (CORES * CHIPS_Y)
        self.me = me
        self.targets = {
            UP: (self.z + 1 < CHIPS_Z, me + CORES * CHIPS_Y),
            DOWN: (self.z > 0, me - CORES * CHIPS_Y),
            ACROSS: (True, self.index(self.z, 1 - self.y, self.core)),
            SIBLING: (True, self.index(self.z, self.y, 1 - self.core)),
        }
        self.pending = []

    def index(self, z, y, core):
        return (z * CHIPS_Y + y) * CORES + core

    def slot(self, which, part, source):
        cut = self.cuts[which]
        start = source * self.shard_rows + (0 if part == FIRST else cut)
        size = cut if part == FIRST else self.shard_rows - cut
        buffer, columns = self.buffers[which]
        return buffer.at[pl.ds(pl.multiple_of(start, 16), size), columns]

    def copy(self, which, part, z, y, core, kind):
        source = self.index(z, y, core)
        block = self.slot(which, part, source)
        return pltpu.make_async_remote_copy(
            src_ref=block,
            dst_ref=block,
            send_sem=self.send_sem.at[which, part, z * CHIPS_Y + y, kind],
            recv_sem=self.recv_sem.at[which, part, source],
            device_id={"wide": self.targets[kind][1]},
            device_id_type=MESH,
        )

    def send(self, which, part, z, y, kinds, valid=True):
        for kind in kinds:
            condition = self.targets[kind][0]
            if condition is True:
                condition = valid
            elif valid is not True:
                condition = jnp.logical_and(condition, valid)
            make = functools.partial(self.copy, which, part, z, y, self.core, kind)
            self.when(condition, lambda make=make: make().start())
            self.pending.append((condition, make))

    def when(self, condition, action):
        if condition is True:
            action()
        else:
            pl.when(condition)(action)

    def arrive(self, which, part, z, y, core, valid=True):
        make = functools.partial(self.copy, which, part, z, y, core, SIBLING)
        self.when(valid, lambda: make().wait_recv())

    def begin_chain(self, which):
        self.send(which, SECOND, self.z, self.y, (ACROSS,))
        self.send(which, FIRST, self.z, self.y, (UP, DOWN))
        self.send(which, SECOND, self.z, self.y, (UP, DOWN))

    def begin_across(self, which):
        self.send(which, FIRST, self.z, self.y, (ACROSS, SIBLING))
        self.send(which, SECOND, self.z, self.y, (SIBLING,))

    def around(self, distance):
        low, high = self.z - distance, self.z + distance
        return ((low, low >= 0, UP), (high, high < CHIPS_Z, DOWN))

    def take_across(self, which, distance):
        y = 1 - self.y
        places = ((self.z, True, None),) if distance == 0 else self.around(distance)
        for z, valid, _ in places:
            self.arrive(which, FIRST, z, y, self.core, valid)
            self.send(which, FIRST, z, y, (SIBLING,), valid)

    def step(self, which, distance):
        if distance == 0:
            y = 1 - self.y
            self.arrive(which, SECOND, self.z, y, self.core)
            self.send(which, SECOND, self.z, y, (UP, DOWN, SIBLING))
            return
        if distance < CHIPS_Z:
            for z, valid, onward in self.around(distance):
                self.arrive(which, FIRST, z, self.y, self.core, valid)
                self.send(which, FIRST, z, self.y, (onward, ACROSS, SIBLING), valid)
            for z, valid, onward in self.around(distance):
                for y in (self.y, 1 - self.y):
                    self.arrive(which, SECOND, z, y, self.core, valid)
                    self.send(which, SECOND, z, y, (onward, SIBLING), valid)
        self.take_across(which, distance - 1)

    def finish(self, which):
        for part in (FIRST, SECOND):
            for z in range(CHIPS_Z):
                for y in range(CHIPS_Y):
                    self.arrive(which, part, z, y, 1 - self.core)

    def drain(self):
        for condition, make in self.pending:
            self.when(condition, lambda make=make: make().wait_send())
        self.pending = []


def fused_kernel(
    lengths_in,
    offsets_in,
    hidden,
    cache,
    w_qkv,
    w_out,
    qkv_bias_in,
    out_bias_in,
    norm_gain_in,
    norm_shift_in,
    hidden_out,
    new_cache,
    lengths,
    offsets,
    qkv_bias,
    out_bias,
    norm_gain,
    norm_shift,
    qkv_rows,
    out_rows,
    cache_here,
    inputs,
    projected,
    attended,
    summed,
    normed,
    scales_all,
    biases,
    stats,
    stats_wide,
    live,
    send_sem,
    recv_sem,
    local_sem,
    side_send,
    side_recv,
):
    tokens, width = hidden.shape
    cache_count = cache.shape[2]
    requests = lengths.shape[0]
    shard_rows = w_out.shape[0]
    heads = width // HEAD
    full_width = 2 * width
    column = lax.axis_index("narrow")
    other = 1 - column
    buffers = [(qkv_rows, slice(kind * width, (kind + 1) * width)) for kind in QKV]
    buffers.append((out_rows, slice(0, width)))
    gather = Gather(buffers, shard_rows, (112, 112, 112, 96), send_sem, recv_sem)

    barrier = pltpu.get_barrier_semaphore()
    for condition, target in gather.targets.values():

        def greet(target=target):
            pl.semaphore_signal(
                barrier, inc=1, device_id={"wide": target}, device_id_type=MESH
            )

        gather.when(condition, greet)
    pl.semaphore_signal(barrier, inc=1, device_id={"narrow": other}, device_id_type=MESH)

    own_rows = pl.ds(pl.multiple_of(gather.me * shard_rows, 16), shard_rows)
    load_qkv = [
        pltpu.make_async_copy(
            w_qkv.at[kind], qkv_rows.at[own_rows, buffers[kind][1]], local_sem.at[9 + kind]
        )
        for kind in QKV
    ]
    load_out = pltpu.make_async_copy(w_out, out_rows.at[own_rows, :], local_sem.at[1])
    load_hidden = pltpu.make_async_copy(hidden, inputs.at[column], local_sem.at[2])
    load_cache = pltpu.make_async_copy(cache, cache_here, local_sem.at[3])
    pairs = (
        (lengths_in, lengths),
        (offsets_in, offsets),
        (qkv_bias_in, qkv_bias),
        (out_bias_in, out_bias),
        (norm_gain_in, norm_gain),
        (norm_shift_in, norm_shift),
    )
    load_small = [
        pltpu.make_async_copy(source, target, local_sem.at[12 + number])
        for number, (source, target) in enumerate(pairs)
    ]
    for load in (*load_qkv, load_hidden, load_out, *load_small, load_cache):
        load.start()

    has_lower = (gather.z + CHIPS_Z - 1) // CHIPS_Z
    has_upper = (2 * CHIPS_Z - 2 - gather.z) // CHIPS_Z
    pl.semaphore_wait(barrier, 3 + has_lower + has_upper)

    def beside(source, target, number):
        return pltpu.make_async_remote_copy(
            src_ref=source,
            dst_ref=target,
            send_sem=side_send.at[number],
            recv_sem=side_recv.at[number],
            device_id={"narrow": other},
            device_id_type=MESH,
        )

    for kind in QKV:
        load_qkv[kind].wait()
        gather.begin_chain(kind)
        gather.begin_across(kind)
    load_hidden.wait()
    for load in load_small:
        load.wait()
    scales_all[column, 0:1, :] = norm_gain[...].astype(jnp.float32).reshape(1, width)
    scales_all[column, 1:2, :] = norm_shift[...].astype(jnp.float32).reshape(1, width)
    scales_all[column, 2:8, :] = jnp.zeros((6, width), jnp.float32)
    biases[0:1, :] = out_bias[...].astype(jnp.float32).reshape(1, width)
    for kind in QKV:
        biases[kind + 1 : kind + 2, :] = qkv_bias[kind : kind + 1, :].astype(jnp.float32)
    send_hidden = beside(inputs.at[column], inputs.at[column], 0)
    send_scales = beside(scales_all.at[column], scales_all.at[column], 1)
    send_hidden.start()
    send_scales.start()
    load_out.wait()
    sides = [send_hidden, send_scales]

    block_start = gather.me * cache_count
    rows_global = block_start + lax.broadcasted_iota(jnp.int32, (8, cache_count), 1)
    for request in range(requests):
        start = offsets[request]
        stop = start + lengths[request]
        alive = jnp.logical_and(rows_global >= start, rows_global < stop)
        live[request] = jnp.where(alive, 0.0, NEGATIVE)
    later = lax.broadcasted_iota(jnp.int32, (SPAN, SPAN), 0) < lax.broadcasted_iota(
        jnp.int32, (SPAN, SPAN), 1
    )
    scale_factor = 1.0 / math.sqrt(HEAD)

    for distance in range(CHIPS_Z):
        for kind in QKV:
            gather.step(kind, distance)
        if distance == CHIPS_Z - 2:
            gather.begin_chain(OUT)
    gather.begin_across(OUT)
    send_hidden.wait_recv()
    send_scales.wait_recv()
    load_cache.wait()

    tile = 512

    def project(layer, source, rows, before):
        for kind in QKV:
            before(kind)

            def one(j, carry, kind=kind):
                here = pl.ds(pl.multiple_of(j * tile, tile), tile)
                columns = pl.ds(pl.multiple_of(kind * width + j * tile, tile), tile)
                total = jnp.dot(
                    source[0, rows, :], qkv_rows[:width, columns], preferred_element_type=jnp.float32
                )
                total += jnp.dot(
                    source[1, rows, :], qkv_rows[width:, columns], preferred_element_type=jnp.float32
                )
                total = total + biases[kind + 1 : kind + 2, here]
                projected[layer, rows, columns] = total.astype(jnp.bfloat16)
                return carry

            lax.fori_loop(0, width // tile, one, 0)

    def store_cache(layer):
        stores = []
        for kind in range(2):
            block = projected.at[layer, :, (kind + 1) * width : (kind + 2) * width]
            store = pltpu.make_async_copy(
                block, new_cache.at[layer, kind], local_sem.at[5 + 2 * layer + kind]
            )
            store.start()
            stores.append(store)
        return stores

    contract = (((1,), (1,)), ((), ()))
    exponent_scale = scale_factor * math.log2(math.e)

    def with_ones(values):
        return jnp.concatenate([values, jnp.ones_like(values)], axis=1)

    def attend_heads(layer, first, count, first_request, last_request):
        span = slice(first_request * SPAN, last_request * SPAN)
        for head in range(first, first + count):
            here = slice(head * HEAD, (head + 1) * HEAD)
            key_columns = slice(width + head * HEAD, width + (head + 1) * HEAD)
            value_columns = slice(2 * width + head * HEAD, 2 * width + (head + 1) * HEAD)
            scores_all = lax.dot_general(
                projected[layer, span, here],
                cache_here[layer, 0, :, here],
                contract,
                preferred_element_type=jnp.float32,
            )
            weights_all, combined_new = [], []
            for request in range(first_request, last_request):
                rows = slice(request * SPAN, (request + 1) * SPAN)
                within = request - first_request
                scores_new = lax.dot_general(
                    projected[layer, rows, here],
                    projected[layer, rows, key_columns],
                    contract,
                    preferred_element_type=jnp.float32,
                )
                scores_cache = scores_all[within * SPAN : (within + 1) * SPAN, :] + live[request, 0:1, :]
                scores_new = jnp.where(later, NEGATIVE, scores_new)
                top = jnp.maximum(
                    jnp.max(scores_cache, axis=1, keepdims=True),
                    jnp.max(scores_new, axis=1, keepdims=True),
                )
                weights_cache = jnp.exp2((scores_cache - top) * exponent_scale)
                weights_new = jnp.exp2((scores_new - top) * exponent_scale)
                weights_all.append(weights_cache.astype(jnp.bfloat16))
                combined_new.append(
                    jnp.dot(
                        weights_new.astype(jnp.bfloat16),
                        with_ones(projected[layer, rows, value_columns]),
                        preferred_element_type=jnp.float32,
                    )
                )
            combined = jnp.dot(
                jnp.concatenate(weights_all, axis=0),
                with_ones(cache_here[layer, 1, :, here]),
                preferred_element_type=jnp.float32,
            )
            combined = combined + jnp.concatenate(combined_new, axis=0)
            combined = combined[:, :HEAD] / combined[:, HEAD:]
            attended[layer, column, span, here] = combined.astype(jnp.bfloat16)

    def share_heads(layer, first, count, rows, number):
        block = attended.at[layer, column, rows, first * HEAD : (first + count) * HEAD]
        copy = beside(block, block, 2 + layer * 4 + number)
        copy.start()
        sides.append(copy)
        return copy

    def mix(layer, carried, rows, after):
        for number in range(width // tile):
            columns = slice(number * tile, (number + 1) * tile)
            total = jnp.dot(
                attended[layer, 0, rows, :],
                out_rows[:width, columns],
                preferred_element_type=jnp.float32,
            )
            total += jnp.dot(
                attended[layer, 1, rows, :],
                out_rows[width:, columns],
                preferred_element_type=jnp.float32,
            )
            total = total + biases[0:1, columns] + carried[column, rows, columns].astype(jnp.float32)
            summed[layer, column, rows, columns] = total.astype(jnp.bfloat16)
            after(number, columns)

    def advance_early(kind):
        gather.step(kind, CHIPS_Z)
        gather.finish(kind)
        if kind == KEY:
            gather.step(OUT, 0)
            gather.step(OUT, 1)

    def advance(number):
        gather.step(OUT, number + 2)

    everything = slice(0, tokens)
    spans = [slice(request * SPAN, (request + 1) * SPAN) for request in range(requests)]
    project(0, inputs, everything, advance_early)
    stores = store_cache(0)
    group = heads // 4
    copies = []
    for number in range(4):
        if number < 3:
            advance(number)
        attend_heads(0, number * group, group, 0, requests)
        copies.append(share_heads(0, number * group, group, everything, number))
    gather.finish(OUT)
    for copy in copies:
        copy.wait_recv()

    exchanged = [[] for _ in spans]
    for request, rows in enumerate(spans):

        def share(number, columns, request=request, rows=rows):
            block = summed.at[0, column, rows, columns]
            copy = beside(block, block, 10 + 2 * request + number)
            copy.start()
            exchanged[request].append(copy)

        mix(0, inputs, rows, share)
    gather.drain()

    chunk = 64

    def norm_rows(j, carry):
        rows = pl.ds(pl.multiple_of(j * chunk, chunk), chunk)
        values = [summed[0, half, rows, :].astype(jnp.float32) for half in range(2)]
        means = sum(jnp.sum(v, axis=1, keepdims=True) for v in values) / full_width
        centered = [v - means for v in values]
        spread = sum(jnp.sum(c * c, axis=1, keepdims=True) for c in centered) / full_width
        inverse = lax.rsqrt(spread + EPSILON)
        for half in range(2):
            scaled = centered[half] * inverse
            scaled = scaled * scales_all[half, 0:1, :] + scales_all[half, 1:2, :]
            normed[half, rows, :] = scaled.astype(jnp.bfloat16)
        return carry


    half_heads = heads // 2
    copies = [[] for _ in spans]
    chunks = SPAN // chunk
    for request, rows in enumerate(spans):
        for copy in exchanged[request]:
            copy.wait_recv()
        sides += exchanged[request]
        lax.fori_loop(request * chunks, (request + 1) * chunks, norm_rows, 0)
        project(1, normed, rows, lambda kind: None)
        for number in range(2):
            attend_heads(1, number * half_heads, half_heads, request, request + 1)
            copies[request].append(
                share_heads(1, number * half_heads, half_heads, rows, 2 * request + number)
            )
    stores += store_cache(1)

    lane = lax.broadcasted_iota(jnp.int32, (chunk, 128), 1)

    def stat_rows(j, carry):
        rows = pl.ds(pl.multiple_of(j * chunk, chunk), chunk)
        values = summed[1, column, rows, :].astype(jnp.float32)
        mean = jnp.sum(values, axis=1, keepdims=True) / width
        centered = values - mean
        spread = jnp.sum(centered * centered, axis=1, keepdims=True)
        stats_wide[0, rows, :] = jnp.where(lane == 0, mean, jnp.where(lane == 1, spread, 0.0))
        return carry

    for request, rows in enumerate(spans):
        for copy in copies[request]:
            copy.wait_recv()
        mix(1, normed, rows, lambda number, columns: None)
        lax.fori_loop(request * chunks, (request + 1) * chunks, stat_rows, 0)
    stats[column] = jnp.transpose(stats_wide[0])[:8, :]
    send_stats = beside(stats.at[column], stats.at[column], 14)
    send_stats.start()
    send_stats.wait_recv()
    sides.append(send_stats)
    for half in range(2):
        padded = jnp.concatenate([stats[half], jnp.zeros((120, tokens), jnp.float32)], axis=0)
        stats_wide[half] = jnp.transpose(padded)

    def last_rows(j, carry):
        rows = pl.ds(pl.multiple_of(j * chunk, chunk), chunk)
        mean_a, mean_b = stats_wide[0, rows, 0:1], stats_wide[1, rows, 0:1]
        means = (mean_a + mean_b) * 0.5
        gap = mean_a - mean_b
        spread = stats_wide[0, rows, 1:2] + stats_wide[1, rows, 1:2] + gap * gap * (width * 0.5)
        inverse = lax.rsqrt(spread / full_width + EPSILON)
        scaled = (summed[1, column, rows, :].astype(jnp.float32) - means) * inverse
        scaled = scaled * scales_all[column, 0:1, :] + scales_all[column, 1:2, :]
        hidden_out[rows, :] = scaled.astype(jnp.bfloat16)
        return carry

    lax.fori_loop(0, tokens // chunk, last_rows, 0)

    for store in stores:
        store.wait()
    for copy in sides:
        copy.wait_send()


def fused(
    hidden_in,
    cache_lengths,
    cache_offsets,
    cache_kv,
    w_qkv,
    qkv_bias,
    w_out,
    out_bias,
    norm_gain,
    norm_shift,
):
    tokens, width = hidden_in.shape
    cache_count = cache_kv.shape[2]
    shard_rows = w_qkv.shape[0]
    depth = shard_rows * lax.axis_size("wide")
    requests = cache_lengths.shape[0]
    vmem = pl.BlockSpec(memory_space=pltpu.VMEM)
    hbm = pl.BlockSpec(memory_space=pltpu.HBM)
    operands = (
        cache_lengths,
        cache_offsets,
        hidden_in,
        cache_kv,
        jnp.transpose(w_qkv, (1, 0, 2)),
        w_out,
        qkv_bias,
        out_bias,
        norm_gain,
        norm_shift,
    )
    anywhere = pl.BlockSpec(memory_space=pl.ANY)
    bf16 = jnp.bfloat16
    return pl.pallas_call(
        fused_kernel,
        out_shape=(
            jax.ShapeDtypeStruct((tokens, width), bf16),
            jax.ShapeDtypeStruct((LAYERS, 2, tokens, width), bf16),
        ),
        in_specs=[hbm] * 10,
        out_specs=(vmem, anywhere),
        scratch_shapes=[
            pltpu.SMEM((requests,), jnp.int32),
            pltpu.SMEM((requests,), jnp.int32),
            pltpu.VMEM((3, width), bf16),
            pltpu.VMEM((width,), bf16),
            pltpu.VMEM((width,), bf16),
            pltpu.VMEM((width,), bf16),
            pltpu.VMEM((depth, 3 * width), bf16),
            pltpu.VMEM((depth, width), bf16),
            pltpu.VMEM((LAYERS, 2, cache_count, width), bf16),
            pltpu.VMEM((2, tokens, width), bf16),
            pltpu.VMEM((LAYERS, tokens, 3 * width), bf16),
            pltpu.VMEM((LAYERS, 2, tokens, width), bf16),
            pltpu.VMEM((LAYERS, 2, tokens, width), bf16),
            pltpu.VMEM((2, tokens, width), bf16),
            pltpu.VMEM((2, 8, width), jnp.float32),
            pltpu.VMEM((8, width), jnp.float32),
            pltpu.VMEM((2, 8, tokens), jnp.float32),
            pltpu.VMEM((2, tokens, 128), jnp.float32),
            pltpu.VMEM((requests, 8, cache_count), jnp.float32),
            pltpu.SemaphoreType.DMA((4, 2, CHIPS_Z * CHIPS_Y, 4)),
            pltpu.SemaphoreType.DMA((4, 2, CHIPS_Z * CHIPS_Y * CORES)),
            pltpu.SemaphoreType.DMA((18,)),
            pltpu.SemaphoreType.DMA((15,)),
            pltpu.SemaphoreType.DMA((15,)),
        ],
        compiler_params=pltpu.CompilerParams(
            collective_id=0, has_side_effects=True, vmem_limit_bytes=VMEM_BYTES
        ),
        cost_estimate=pl.CostEstimate(
            flops=2 * LAYERS * tokens * depth * 4 * width,
            bytes_accessed=2 * depth * 4 * width,
            transcendentals=LAYERS * tokens * cache_count * (width // HEAD),
        ),
    )(*(pltpu.with_memory_space_constraint(operand, pltpu.HBM) for operand in operands))


def solution(mesh):
    in_specs = (
        P("wide", "narrow"),
        P("wide"),
        P("wide"),
        P(None, None, "wide", "narrow"),
        P("wide", None, "narrow"),
        P(None, "narrow"),
        P("wide", "narrow"),
        P("narrow"),
        P("narrow"),
        P("narrow"),
    )
    out_specs = (P("wide", "narrow"), P(None, None, "wide", "narrow"))
    body = fused if fits_fused(mesh) else shards
    return jax.shard_map(body, mesh=mesh, in_specs=in_specs, out_specs=out_specs, check_vma=False)
```
